32 devices in a mesh: lon: 8 (over y, x, core), lat: 4 (over z).
Axes of the slice: x: 2, y: 2, z: 4, core: 2. Of those that a mesh axis runs over, the one named last changes fastest.
Arguments:
- tracer: float32 [8, 512, 2048], P(None, 'lat', 'lon'), may hold values from -8 to 8
- courant: float32 [8, 512, 2048], P(None, 'lat', 'lon'), may hold values from 0.25 to 10240
- hop_counts: int32 [512], P('lat'), may hold values from 0 to 7, as said below
- row_area: float32 [512], P('lat'), may hold values from 1 to 10
Outputs:
- updated: float32 [8, 512, 2048], P(None, 'lat', 'lon')
- dateline_flux: float32 [8], replicated
The draws below stay inside these ranges and needn't reach their ends.
Inputs may be any that keep to these rules, and one draw needn't show every extreme that they name: `hop_counts`: only the first 8 and the last 8 latitude rows may have counts above 0.
All inputs are finite; a program needn't handle non-finite values.
Results may differ from the reference program's by a relative error of at most 0.0003.
Values sent between devices are 32-bit elements; how exact they have to be, the bound alone decides.
A program may use at most 64 MiB of HBM per device.

```python
import math
import jax
import jax.numpy as jnp
from jax import lax

CELLS = 256
VERTICAL_LAYERS = 8
POLAR = 8
STOPS = 7
LONGITUDE_COUNT = 2048
LATITUDE_ROWS = 512


def draw_tracer(key, part):
    first = jax.random.fold_in(key, 0)
    values = jax.random.normal(first, (VERTICAL_LAYERS, LATITUDE_ROWS, LONGITUDE_COUNT), jnp.float32)
    return jnp.clip(values, -8.0, 8.0)


def draw_courant(key, part):
    random_keys = jax.random.split(key, 7)
    starting_point = jnp.exp(jax.random.uniform(random_keys[1], (VERTICAL_LAYERS, LATITUDE_ROWS, 1), jnp.float32, jnp.log(0.5), jnp.log(5.0)))
    rows = jnp.arange(LATITUDE_ROWS, dtype=jnp.float32)
    latitude = (rows + 0.5) / LATITUDE_ROWS * jnp.pi - 0.5 * jnp.pi
    broaden_range = 1.0 / jnp.cos(latitude)
    coarse_estimate = jax.random.uniform(random_keys[3], (VERTICAL_LAYERS, LATITUDE_ROWS, LONGITUDE_COUNT), jnp.float32, 0.5, 1.5)
    row_index = jnp.arange(LATITUDE_ROWS, dtype=jnp.int32)
    polar_rows = (row_index < POLAR) | (row_index >= LATITUDE_ROWS - POLAR)
    polar_factor = jax.random.uniform(random_keys[6], (VERTICAL_LAYERS, LATITUDE_ROWS, 1), jnp.float32, 1.0, 2.0)
    polar_value = LONGITUDE_COUNT * polar_factor * coarse_estimate
    drawn_value = starting_point * coarse_estimate * broaden_range[None, :, None]
    base_value = jnp.where(polar_rows[None, :, None], polar_value, drawn_value)
    cell_positions = jax.random.randint(random_keys[4], (VERTICAL_LAYERS, LATITUDE_ROWS, 2), 0, LONGITUDE_COUNT)
    grid_cells = jnp.arange(LONGITUDE_COUNT, dtype=jnp.int32)[None, None, :]
    sudden_release = (grid_cells == cell_positions[:, :, 0:1]) | (grid_cells == cell_positions[:, :, 1:2])
    release_value = jax.random.uniform(random_keys[5], (VERTICAL_LAYERS, LATITUDE_ROWS, LONGITUDE_COUNT), jnp.float32, 1.0, 4.0)
    return jnp.where(sudden_release, release_value, base_value)


def draw_hop_counts(key, part):
    values = jax.random.randint(key, (LATITUDE_ROWS,), 0, STOPS + 1)
    rows = jnp.arange(LATITUDE_ROWS, dtype=jnp.int32)
    polar = (rows < POLAR) | (rows >= LATITUDE_ROWS - POLAR)
    values = jnp.where(polar, values, 0)
    return jnp.where(rows == 0, STOPS, values).astype(jnp.int32)


def shard_levels(rng, extent, pieces, smallest, high):
    factor_of, own = 1.0, jax.random.fold_in(rng, 6)
    for position, blocks in pieces:
        draws = jnp.exp(jax.random.uniform(jax.random.fold_in(own, position), (blocks,), jnp.float32, smallest / len(pieces), high / len(pieces)))
        factor_of = factor_of * jnp.repeat(draws, extent[position] // blocks).reshape([-1 if axis == position else 1 for axis in range(len(extent))])
    return factor_of


def setup_inputs(seed: int = 0) -> dict:
    splits = jax.random.split(jax.random.key(seed), 5)
    return {
        "tracer": draw_tracer(jax.random.fold_in(splits[4], 71), 0),
        "courant": draw_courant(jax.random.fold_in(splits[4], 71), 0),
        "hop_counts": draw_hop_counts(jax.random.fold_in(splits[4], 71), 0),
        "row_area": jnp.clip(jnp.exp(math.log(10.0) - 2.3025851 * jax.random.uniform(splits[3], (LATITUDE_ROWS,), jnp.float32) ** shard_levels(splits[3], (LATITUDE_ROWS,), ((0, 4),), -0.2, 0.2)), 1.0, 10.0),
    }


def roll_rows(rows, amount):
    return jnp.roll(rows, amount, axis=-1)


def reference(tracer, courant, hop_counts, row_area):
    amounts = (hop_counts * CELLS).astype(jnp.int32)
    shifted = jax.vmap(roll_rows, in_axes=(1, 0), out_axes=1)(tracer, amounts)
    ratios = courant / (1.0 + courant)
    source_t = jnp.moveaxis(shifted, 2, 0)
    ratios_t = jnp.moveaxis(ratios, 2, 0)

    def first_pass(state_pair, inputs):
        source, factor = inputs
        return (state_pair[0] * factor, factor * (source + state_pair[1])), None

    ones = jnp.ones(tracer.shape[:2], jnp.float32)
    zeros = jnp.zeros(tracer.shape[:2], jnp.float32)
    (growth, offset), unused = lax.scan(first_pass, (ones, zeros), (source_t, ratios_t))
    wrap = offset / (1.0 - growth)

    def second_pass(inflow, inputs):
        source, factor = inputs
        return factor * (source + inflow), inflow

    unused_last, before = lax.scan(second_pass, wrap, (source_t, ratios_t))
    updated = (shifted + jnp.moveaxis(before, 0, 2)) / (1.0 + courant)
    dateline_flux = jnp.sum(row_area[None, :] * wrap, axis=1) / jnp.sum(row_area)
    return updated, dateline_flux
```

```python
import functools

import jax
import jax.numpy as jnp
from jax import lax
from jax.experimental import pallas as pl
from jax.experimental.pallas import tpu as pltpu
from jax.sharding import PartitionSpec as P

POLAR = 8
STOPS = 7
LANES = 128
CHUNK = 32


def lane_index(shape):
    return lax.broadcasted_iota(jnp.int32, shape, len(shape) - 1)


def scan_lanes(growth, offset):
    lane = lane_index(growth.shape)
    stride = 1
    while stride < LANES:
        inside = lane >= stride
        lead_growth = pltpu.roll(growth, stride, 1)
        lead_offset = pltpu.roll(offset, stride, 1)
        offset = jnp.where(inside, growth * lead_offset + offset, offset)
        growth = jnp.where(inside, growth * lead_growth, growth)
        stride *= 2
    return growth, offset


def solve_block(courants, sources):
    out, end = [], None
    for courant, source in zip(courants, sources):
        above = 1.0 + courant
        shared = 1.0 / (courant * above)
        ratio = 1.0 - shared * courant
        inverse = shared * above
        growth, offset = scan_lanes(ratio, ratio * source)
        if end is not None:
            offset = growth * end[1] + offset
            growth = growth * end[0]
        end = (
            jnp.broadcast_to(growth[:, LANES - 1 :], growth.shape),
            jnp.broadcast_to(offset[:, LANES - 1 :], offset.shape),
        )
        out.append((growth * inverse, offset * inverse))
    return out, end


def kernel(
    n, z, tracer, courant, hops, area, updated, dateline,
    trv, cov, ends, maps, pt, pc, pu, back, part,
    in_sem, own_sem, p_send, p_recv, m_send, m_recv, b_send, b_recv, d_send, d_recv,
):
    levels, rows, cells = trv.shape
    halves = cells // LANES
    me = lax.axis_index("lon")
    lat = lax.axis_index("lat")
    polar = (lat == 0) | (lat == z - 1)
    row0 = pl.multiple_of(jnp.where(lat == 0, 0, rows - POLAR), POLAR)
    slab = pl.ds(row0, POLAR)

    def ahead(k):
        return lax.rem(me + k, n)

    def behind(k):
        return lax.rem(me + n - k, n)

    def is_worker(device, work):
        if n == levels:
            work()
        else:
            pl.when(device < levels)(work)

    barrier = pltpu.get_barrier_semaphore()
    for k in range(1, n):
        pl.semaphore_signal(barrier, inc=1, device_id={"lon": ahead(k)}, device_id_type=pl.DeviceIdType.MESH)
    for k in range(1, z):
        pl.semaphore_signal(
            barrier, inc=1, device_id={"lat": lax.rem(lat + k, z)}, device_id_type=pl.DeviceIdType.MESH
        )

    def load(l):
        return (
            pltpu.make_async_copy(tracer.at[l], trv.at[l], in_sem.at[0, l]),
            pltpu.make_async_copy(courant.at[l], cov.at[l], in_sem.at[1, l]),
        )

    for l in range(levels):
        for copy in load(l):
            copy.start()

    def remote(source, target, send, recv, k, axis="lon"):
        place = ahead(k) if axis == "lon" else lax.rem(lat + k, z)
        return pltpu.make_async_remote_copy(
            src_ref=source, dst_ref=target, send_sem=send, recv_sem=recv,
            device_id={axis: place}, device_id_type=pl.DeviceIdType.MESH,
        )

    def polar_out(k):
        level = lax.rem(ahead(k), levels)
        return (
            remote(courant.at[level, slab], pc.at[me], p_send.at[0, k], p_recv.at[0, k], k),
            remote(tracer.at[level, slab], pt.at[me], p_send.at[1, k], p_recv.at[1, k], k),
        )

    def polar_own():
        level = lax.rem(me, levels)
        return (
            pltpu.make_async_copy(courant.at[level, slab], pc.at[me], own_sem.at[0]),
            pltpu.make_async_copy(tracer.at[level, slab], pt.at[me], own_sem.at[1]),
        )

    pl.semaphore_wait(barrier, n + z - 2)

    @pl.when(polar)
    def _():
        for k in range(1, n):
            def send(k=k):
                for copy in polar_out(k):
                    copy.start()
            is_worker(ahead(k), send)

        def own():
            for copy in polar_own():
                copy.start()
        is_worker(me, own)

    @pl.loop(0, levels)
    def _(l):
        for copy in load(l):
            copy.wait()
        for first in range(0, rows, CHUNK):
            part_rows = pl.ds(first, CHUNK)
            columns = [pl.ds(h * LANES, LANES) for h in range(halves)]
            out, end = solve_block(
                [cov[l, part_rows, c] for c in columns], [trv[l, part_rows, c] for c in columns]
            )
            for c, (growth, offset) in zip(columns, out):
                cov[l, part_rows, c] = growth
                trv[l, part_rows, c] = offset
            lane = lane_index((CHUNK, LANES))
            held = jnp.where(lane == l, end[0], ends[part_rows, :])
            ends[part_rows, :] = jnp.where(lane == l + levels, end[1], held)

    maps[me] = jnp.transpose(ends[...])[: 2 * levels]

    def map_out(k):
        return remote(maps.at[me], maps.at[me], m_send.at[k], m_recv.at[k], k)

    for k in range(1, n):
        map_out(k).start()

    lane = lane_index((POLAR, LANES))
    sublane = lax.broadcasted_iota(jnp.int32, (POLAR, LANES), 0)

    def back_out(k):
        return remote(
            pu.at[ahead(k)], back.at[lax.rem(me, levels)], b_send.at[k], b_recv.at[k], k
        )

    def column(values):
        place = lane_index((POLAR, rows)) == lax.broadcasted_iota(jnp.int32, (POLAR, rows), 0) + row0
        return jnp.sum(jnp.where(place, jnp.broadcast_to(values, (POLAR, rows)), 0.0), axis=1, keepdims=True)

    def solve_polar():
        for k in range(1, n):
            for copy in polar_out(k):
                copy.wait_recv()
        for copy in polar_own():
            copy.wait()
        count = jnp.broadcast_to(column(hops[...].astype(jnp.float32)), (POLAR, LANES)).astype(jnp.int32)
        courants, sources = [], []
        for h in range(halves):
            c = pl.ds(h * LANES, LANES)
            blocks = [pt[s, :, c] for s in range(n)]
            for bit in range(STOPS.bit_length()):
                chosen = jnp.right_shift(count, bit) % 2 == 1
                blocks = [
                    jnp.where(chosen, blocks[(s - (1 << bit)) % n], blocks[s]) for s in range(n)
                ]
            sources.append(jnp.concatenate(blocks, axis=0))
            courants.append(jnp.concatenate([pc[s, :, c] for s in range(n)], axis=0))
        out, end = solve_block(courants, sources)
        growth = jnp.ones((POLAR, LANES), jnp.float32)
        offset = jnp.zeros((POLAR, LANES), jnp.float32)
        prior = []
        for s in range(n):
            prior.append((growth, offset))
            own = slice(s * POLAR, (s + 1) * POLAR)
            offset = end[0][own] * offset + end[1][own]
            growth = growth * end[0][own]
        wrap = offset / (1.0 - growth)
        weighted = jnp.sum(column(area[...]) * wrap, axis=0, keepdims=True)
        weighted = jnp.broadcast_to(weighted, (POLAR, LANES))
        for s in range(n):
            inflow = prior[s][0] * wrap + prior[s][1]
            own = slice(s * POLAR, (s + 1) * POLAR)
            for h, (g, o) in enumerate(out):
                c = pl.ds(h * LANES, LANES)
                pu[s, :POLAR, c] = g[own] * inflow + o[own]
                pu[s, POLAR:, c] = weighted
        for k in range(1, n):
            back_out(k).start()
        back[lax.rem(me, levels)] = pu[me]

    @pl.when(polar)
    def _():
        is_worker(me, solve_polar)

    for k in range(1, n):
        map_out(k).wait_recv()
    growth = jnp.ones((levels, rows), jnp.float32)
    offset = jnp.zeros((levels, rows), jnp.float32)
    prior_growth, prior_offset = growth, offset
    for s in range(n):
        here = s == me
        prior_growth = jnp.where(here, growth, prior_growth)
        prior_offset = jnp.where(here, offset, prior_offset)
        own = maps[s]
        offset = own[:levels] * offset + own[levels:]
        growth = growth * own[:levels]
    wrap = offset / (1.0 - growth)
    inflow = prior_growth * wrap + prior_offset
    spread = jnp.transpose(jnp.concatenate([inflow] * (LANES // levels), axis=0))

    areas = jnp.broadcast_to(area[...], (levels, rows))
    row = lane_index((levels, rows))
    masked = polar & (row >= row0) & (row < row0 + POLAR)
    part[lat, :levels] = jnp.where(masked, 0.0, areas * wrap)
    part[lat, levels:] = areas

    for l in range(levels):
        for first in range(0, rows, CHUNK):
            part_rows = pl.ds(first, CHUNK)
            level_inflow = jnp.broadcast_to(spread[first : first + CHUNK, l : l + 1], (CHUNK, LANES))
            for h in range(halves):
                c = pl.ds(h * LANES, LANES)
                updated[l, part_rows, c] = cov[l, part_rows, c] * level_inflow + trv[l, part_rows, c]

    def part_out(k):
        return remote(part.at[lat], part.at[lat], d_send.at[k], d_recv.at[k], k, "lat")

    @pl.when(polar)
    def _():
        for k in range(1, n):
            def receive(k=k):
                back_out(k).wait_recv()
            is_worker(behind(k), receive)
        total = jnp.zeros((levels, LANES), jnp.float32)
        sub = lax.broadcasted_iota(jnp.int32, (levels, LANES), 0)
        for l in range(levels):
            total = jnp.where(sub == l, back[l, POLAR : POLAR + 1, :LANES], total)
        first_lane = lane_index((levels, LANES)) == 0
        part[lat, :levels, :LANES] = part[lat, :levels, :LANES] + jnp.where(first_lane, total, 0.0)

    for k in range(1, z):
        part_out(k).start()

    @pl.when(polar)
    def _():
        for l in range(levels):
            updated[l, slab, :] = back[l, :POLAR, :]

    for k in range(1, z):
        part_out(k).wait_recv()
    total = part[0]
    for s in range(1, z):
        total = total + part[s]
    sums = jnp.sum(total, axis=1, keepdims=True)
    mean = jnp.broadcast_to(sums[:levels] / sums[levels:], (levels, LANES))
    diagonal = lax.broadcasted_iota(jnp.int32, (levels, LANES), 0) == lane_index((levels, LANES))
    dateline[...] = jnp.sum(jnp.where(diagonal, mean, 0.0), axis=0, keepdims=True)[:, :levels]

    for k in range(1, z):
        part_out(k).wait_send()
    for k in range(1, n):
        map_out(k).wait_send()

    @pl.when(polar)
    def _():
        for k in range(1, n):
            def sent(k=k):
                for copy in polar_out(k):
                    copy.wait_send()
            is_worker(ahead(k), sent)

        def returned():
            for k in range(1, n):
                back_out(k).wait_send()
        is_worker(me, returned)


def body(n, z, tracer, courant, hop_counts, row_area):
    levels, rows, cells = tracer.shape
    f32 = jnp.float32
    vmem = pl.BlockSpec(memory_space=pltpu.VMEM)
    hbm = pl.BlockSpec(memory_space=pl.ANY)
    dma = pltpu.SemaphoreType.DMA
    updated, dateline = pl.pallas_call(
        functools.partial(kernel, n, z),
        out_shape=(
            jax.ShapeDtypeStruct(tracer.shape, f32),
            jax.ShapeDtypeStruct((1, levels), f32),
        ),
        in_specs=[hbm, hbm, vmem, vmem],
        out_specs=(vmem, vmem),
        scratch_shapes=[
            pltpu.VMEM(tracer.shape, f32),
            pltpu.VMEM(tracer.shape, f32),
            pltpu.VMEM((rows, LANES), f32),
            pltpu.VMEM((n, 2 * levels, rows), f32),
            pltpu.VMEM((n, POLAR, cells), f32),
            pltpu.VMEM((n, POLAR, cells), f32),
            pltpu.VMEM((n, 2 * POLAR, cells), f32),
            pltpu.VMEM((levels, 2 * POLAR, cells), f32),
            pltpu.VMEM((z, 2 * levels, rows), f32),
            dma((2, levels)), dma((2,)),
            dma((2, n)), dma((2, n)),
            dma((n,)), dma((n,)),
            dma((n,)), dma((n,)),
            dma((z,)), dma((z,)),
        ],
        compiler_params=pltpu.CompilerParams(
            collective_id=0, has_side_effects=True, vmem_limit_bytes=16 * 1024 * 1024
        ),
        cost_estimate=pl.CostEstimate(
            flops=60 * tracer.size, bytes_accessed=12 * tracer.size, transcendentals=tracer.size
        ),
    )(tracer, courant, hop_counts.reshape(1, rows), row_area.reshape(1, rows))
    return updated, dateline.reshape(levels)


def solution(mesh):
    return jax.shard_map(
        functools.partial(body, mesh.shape["lon"], mesh.shape["lat"]),
        mesh=mesh,
        in_specs=(P(None, "lat", "lon"), P(None, "lat", "lon"), P("lat"), P("lat")),
        out_specs=(P(None, "lat", "lon"), P()),
        check_vma=False,
    )
```

```python
import functools

import jax
import jax.numpy as jnp
from jax import lax
from jax.experimental import pallas as pl
from jax.experimental.pallas import tpu as pltpu
from jax.sharding import PartitionSpec as P

POLAR = 8
STOPS = 7
LANES = 128
CHUNKS = 8


def lane_index(shape):
    return lax.broadcasted_iota(jnp.int32, shape, len(shape) - 1)


def scan_lanes(growth, offset):
    lane = lane_index(growth.shape)
    stride = 1
    while stride < LANES:
        inside = lane >= stride
        lead_growth = pltpu.roll(growth, stride, 1)
        lead_offset = pltpu.roll(offset, stride, 1)
        offset = jnp.where(inside, growth * lead_offset + offset, offset)
        growth = jnp.where(inside, growth * lead_growth, growth)
        stride *= 2
    return growth, offset


def solve_block(courants, sources):
    out, end = [], None
    for courant, source in zip(courants, sources):
        above = 1.0 + courant
        shared = 1.0 / (courant * above)
        ratio = 1.0 - shared * courant
        inverse = shared * above
        growth, offset = scan_lanes(ratio, ratio * source)
        if end is not None:
            offset = growth * end[1] + offset
            growth = growth * end[0]
        end = (
            jnp.broadcast_to(growth[:, LANES - 1 :], growth.shape),
            jnp.broadcast_to(offset[:, LANES - 1 :], offset.shape),
        )
        out.append((growth * inverse, offset * inverse))
    return out, end


def kernel(
    n, z, tracer, courant, hops_in, area_in, updated, dateline,
    trv, cov, st, ct, gs, os, maps, pt, pc, pu, back, part,
    hops, area, small_sem, in_sem, own_sem, p_send, p_recv, m_send, m_recv, b_send, b_recv, d_send, d_recv,
):
    levels, rows, cells = trv.shape
    halves = cells // LANES
    me = lax.axis_index("lon")
    lat = lax.axis_index("lat")
    polar = (lat == 0) | (lat == z - 1)
    row0 = pl.multiple_of(jnp.where(lat == 0, 0, rows - POLAR), POLAR)
    slab = pl.ds(row0, POLAR)

    def ahead(k):
        return lax.rem(me + k, n)

    def behind(k):
        return lax.rem(me + n - k, n)

    def is_worker(device, work):
        if n == levels:
            work()
        else:
            pl.when(device < levels)(work)

    barrier = pltpu.get_barrier_semaphore()
    for k in range(1, n):
        pl.semaphore_signal(barrier, inc=1, device_id={"lon": ahead(k)}, device_id_type=pl.DeviceIdType.MESH)
    for k in range(1, z):
        pl.semaphore_signal(
            barrier, inc=1, device_id={"lat": lax.rem(lat + k, z)}, device_id_type=pl.DeviceIdType.MESH
        )

    def load(l):
        return (
            pltpu.make_async_copy(tracer.at[l], trv.at[l], in_sem.at[0, l]),
            pltpu.make_async_copy(courant.at[l], cov.at[l], in_sem.at[1, l]),
        )

    for l in range(levels):
        for copy in load(l):
            copy.start()
    small = (
        pltpu.make_async_copy(hops_in, hops, small_sem.at[0]),
        pltpu.make_async_copy(area_in, area, small_sem.at[1]),
    )
    for copy in small:
        copy.start()

    def remote(source, target, send, recv, k, axis="lon"):
        place = ahead(k) if axis == "lon" else lax.rem(lat + k, z)
        return pltpu.make_async_remote_copy(
            src_ref=source, dst_ref=target, send_sem=send, recv_sem=recv,
            device_id={axis: place}, device_id_type=pl.DeviceIdType.MESH,
        )

    def polar_out(k):
        level = lax.rem(ahead(k), levels)
        return (
            remote(courant.at[level, slab], pc.at[me], p_send.at[0, k], p_recv.at[0, k], k),
            remote(tracer.at[level, slab], pt.at[me], p_send.at[1, k], p_recv.at[1, k], k),
        )

    def polar_own():
        level = lax.rem(me, levels)
        return (
            pltpu.make_async_copy(courant.at[level, slab], pc.at[me], own_sem.at[0]),
            pltpu.make_async_copy(tracer.at[level, slab], pt.at[me], own_sem.at[1]),
        )

    pl.semaphore_wait(barrier, n + z - 2)

    @pl.when(polar)
    def _():
        for k in range(1, n):
            def send(k=k):
                for copy in polar_out(k):
                    copy.start()
            is_worker(ahead(k), send)

        def own():
            for copy in polar_own():
                copy.start()
        is_worker(me, own)

    @pl.loop(0, levels)
    def _(l):
        for copy in load(l):
            copy.wait()
        for h in range(halves):
            c = pl.ds(h * LANES, LANES)
            ct[l, c, :] = jnp.transpose(cov[l, :, c])
            st[l, c, :] = jnp.transpose(trv[l, :, c])

    for copy in small:
        copy.wait()
    steps = cells // CHUNKS

    def step(v, state):
        growth, offset = state
        cells_v = pl.ds(v, CHUNKS, stride=steps)
        here, source = ct[:, cells_v, :], st[:, cells_v, :]
        above = 1.0 + here
        shared = 1.0 / (here * above)
        ratio = 1.0 - shared * here
        inverse = shared * above
        growth = growth * ratio
        offset = ratio * source + ratio * offset
        gs[v] = growth * inverse
        os[v] = offset * inverse
        return growth, offset

    shape = (levels, CHUNKS, rows)
    growth, offset = lax.fori_loop(
        0, steps, step, (jnp.ones(shape, jnp.float32), jnp.zeros(shape, jnp.float32)), unroll=4
    )
    sub = lax.broadcasted_iota(jnp.int32, (CHUNKS, rows), 0)
    before = []
    for l in range(levels):
        g, o = growth[l], offset[l]
        stride = 1
        while stride < CHUNKS:
            inside = sub >= stride
            lead_g, lead_o = pltpu.roll(g, stride, 0), pltpu.roll(o, stride, 0)
            o = jnp.where(inside, g * lead_o + o, o)
            g = jnp.where(inside, g * lead_g, g)
            stride *= 2
        maps[me, l : l + 1, :] = g[CHUNKS - 1 :]
        maps[me, levels + l : levels + l + 1, :] = o[CHUNKS - 1 :]
        before.append(
            (jnp.where(sub == 0, 1.0, pltpu.roll(g, 1, 0)), jnp.where(sub == 0, 0.0, pltpu.roll(o, 1, 0)))
        )

    def map_out(k):
        return remote(maps.at[me], maps.at[me], m_send.at[k], m_recv.at[k], k)

    for k in range(1, n):
        map_out(k).start()

    lane = lane_index((POLAR, LANES))
    sublane = lax.broadcasted_iota(jnp.int32, (POLAR, LANES), 0)

    def back_out(k):
        return remote(
            pu.at[ahead(k)], back.at[lax.rem(me, levels)], b_send.at[k], b_recv.at[k], k
        )

    def column(values):
        place = lane_index((POLAR, rows)) == lax.broadcasted_iota(jnp.int32, (POLAR, rows), 0) + row0
        return jnp.sum(jnp.where(place, jnp.broadcast_to(values, (POLAR, rows)), 0.0), axis=1, keepdims=True)

    def solve_polar():
        for k in range(1, n):
            for copy in polar_out(k):
                copy.wait_recv()
        for copy in polar_own():
            copy.wait()
        count = jnp.broadcast_to(column(hops[...].astype(jnp.float32)), (POLAR, LANES)).astype(jnp.int32)
        courants, sources = [], []
        for h in range(halves):
            c = pl.ds(h * LANES, LANES)
            blocks = [pt[s, :, c] for s in range(n)]
            for bit in range(STOPS.bit_length()):
                chosen = jnp.right_shift(count, bit) % 2 == 1
                blocks = [
                    jnp.where(chosen, blocks[(s - (1 << bit)) % n], blocks[s]) for s in range(n)
                ]
            sources.append(jnp.concatenate(blocks, axis=0))
            courants.append(jnp.concatenate([pc[s, :, c] for s in range(n)], axis=0))
        out, end = solve_block(courants, sources)
        growth = jnp.ones((POLAR, LANES), jnp.float32)
        offset = jnp.zeros((POLAR, LANES), jnp.float32)
        prior = []
        for s in range(n):
            prior.append((growth, offset))
            own = slice(s * POLAR, (s + 1) * POLAR)
            offset = end[0][own] * offset + end[1][own]
            growth = growth * end[0][own]
        wrap = offset / (1.0 - growth)
        weighted = jnp.sum(column(area[...]) * wrap, axis=0, keepdims=True)
        weighted = jnp.broadcast_to(weighted, (POLAR, LANES))
        for s in range(n):
            inflow = prior[s][0] * wrap + prior[s][1]
            own = slice(s * POLAR, (s + 1) * POLAR)
            for h, (g, o) in enumerate(out):
                c = pl.ds(h * LANES, LANES)
                pu[s, :POLAR, c] = g[own] * inflow + o[own]
                pu[s, POLAR:, c] = weighted
        for k in range(1, n):
            back_out(k).start()
        back[lax.rem(me, levels)] = pu[me]

    @pl.when(polar)
    def _():
        is_worker(me, solve_polar)

    for k in range(1, n):
        map_out(k).wait_recv()
    growth = jnp.ones((levels, rows), jnp.float32)
    offset = jnp.zeros((levels, rows), jnp.float32)
    prior_growth, prior_offset = growth, offset
    for s in range(n):
        here = s == me
        prior_growth = jnp.where(here, growth, prior_growth)
        prior_offset = jnp.where(here, offset, prior_offset)
        own = maps[s]
        offset = own[:levels] * offset + own[levels:]
        growth = growth * own[:levels]
    wrap = offset / (1.0 - growth)
    inflow = prior_growth * wrap + prior_offset
    areas = jnp.broadcast_to(area[...], (levels, rows))
    row = lane_index((levels, rows))
    masked = polar & (row >= row0) & (row < row0 + POLAR)
    part[lat, :levels] = jnp.where(masked, 0.0, areas * wrap)
    part[lat, levels:] = areas

    inflows = jnp.stack([before[l][0] * inflow[l : l + 1] + before[l][1] for l in range(levels)])

    def apply(v, carry):
        ct[:, pl.ds(v, CHUNKS, stride=steps), :] = gs[v] * inflows + os[v]
        return carry

    lax.fori_loop(0, steps, apply, 0, unroll=4)

    @pl.loop(0, levels)
    def _(l):
        for h in range(halves):
            c = pl.ds(h * LANES, LANES)
            updated[l, :, c] = jnp.transpose(ct[l, c, :])

    def part_out(k):
        return remote(part.at[lat], part.at[lat], d_send.at[k], d_recv.at[k], k, "lat")

    @pl.when(polar)
    def _():
        for k in range(1, n):
            def receive(k=k):
                back_out(k).wait_recv()
            is_worker(behind(k), receive)
        total = jnp.zeros((levels, LANES), jnp.float32)
        sub = lax.broadcasted_iota(jnp.int32, (levels, LANES), 0)
        for l in range(levels):
            total = jnp.where(sub == l, back[l, POLAR : POLAR + 1, :LANES], total)
        first_lane = lane_index((levels, LANES)) == 0
        part[lat, :levels, :LANES] = part[lat, :levels, :LANES] + jnp.where(first_lane, total, 0.0)

    for k in range(1, z):
        part_out(k).start()

    @pl.when(polar)
    def _():
        for l in range(levels):
            updated[l, slab, :] = back[l, :POLAR, :]

    for k in range(1, z):
        part_out(k).wait_recv()
    total = part[0]
    for s in range(1, z):
        total = total + part[s]
    sums = jnp.sum(total, axis=1, keepdims=True)
    mean = jnp.broadcast_to(sums[:levels] / sums[levels:], (levels, LANES))
    diagonal = lax.broadcasted_iota(jnp.int32, (levels, LANES), 0) == lane_index((levels, LANES))
    dateline[...] = jnp.sum(jnp.where(diagonal, mean, 0.0), axis=0, keepdims=True)[:, :levels]

    for k in range(1, z):
        part_out(k).wait_send()
    for k in range(1, n):
        map_out(k).wait_send()

    @pl.when(polar)
    def _():
        for k in range(1, n):
            def sent(k=k):
                for copy in polar_out(k):
                    copy.wait_send()
            is_worker(ahead(k), sent)

        def returned():
            for k in range(1, n):
                back_out(k).wait_send()
        is_worker(me, returned)


def body(n, z, tracer, courant, hop_counts, row_area):
    levels, rows, cells = tracer.shape
    f32 = jnp.float32
    vmem = pl.BlockSpec(memory_space=pltpu.VMEM)
    hbm = pl.BlockSpec(memory_space=pl.ANY)
    dma = pltpu.SemaphoreType.DMA
    inputs = (tracer, courant, hop_counts.reshape(1, rows), row_area.reshape(1, rows))
    updated, dateline = pl.pallas_call(
        functools.partial(kernel, n, z),
        out_shape=(
            pltpu.VMEM(tracer.shape, f32),
            pltpu.VMEM((1, levels), f32),
        ),
        in_specs=[hbm] * 4,
        out_specs=(vmem, vmem),
        scratch_shapes=[
            pltpu.VMEM(tracer.shape, f32),
            pltpu.VMEM(tracer.shape, f32),
            pltpu.VMEM((levels, cells, rows), f32),
            pltpu.VMEM((levels, cells, rows), f32),
            pltpu.VMEM((cells // CHUNKS, levels, CHUNKS, rows), f32),
            pltpu.VMEM((cells // CHUNKS, levels, CHUNKS, rows), f32),
            pltpu.VMEM((n, 2 * levels, rows), f32),
            pltpu.VMEM((n, POLAR, cells), f32),
            pltpu.VMEM((n, POLAR, cells), f32),
            pltpu.VMEM((n, 2 * POLAR, cells), f32),
            pltpu.VMEM((levels, 2 * POLAR, cells), f32),
            pltpu.VMEM((z, 2 * levels, rows), f32),
            pltpu.VMEM((1, rows), jnp.int32),
            pltpu.VMEM((1, rows), f32),
            dma((2,)), dma((2, levels)), dma((2,)),
            dma((2, n)), dma((2, n)),
            dma((n,)), dma((n,)),
            dma((n,)), dma((n,)),
            dma((z,)), dma((z,)),
        ],
        compiler_params=pltpu.CompilerParams(
            collective_id=0, has_side_effects=True, vmem_limit_bytes=24 * 1024 * 1024
        ),
        cost_estimate=pl.CostEstimate(
            flops=60 * tracer.size, bytes_accessed=12 * tracer.size, transcendentals=tracer.size
        ),
    )(*(pltpu.with_memory_space_constraint(a, pltpu.HBM) for a in inputs))
    return updated, dateline.reshape(levels)


def solution(mesh):
    return jax.shard_map(
        functools.partial(body, mesh.shape["lon"], mesh.shape["lat"]),
        mesh=mesh,
        in_specs=(P(None, "lat", "lon"), P(None, "lat", "lon"), P("lat"), P("lat")),
        out_specs=(P(None, "lat", "lon"), P()),
        check_vma=False,
    )
```

```python
import functools

import jax
import jax.numpy as jnp
from jax import lax
from jax.experimental import pallas as pl
from jax.experimental.pallas import tpu as pltpu
from jax.sharding import PartitionSpec as P

POLAR = 8
STOPS = 7
LANES = 128
CHUNKS = 8
GROUP = 2


def lane_index(shape):
    return lax.broadcasted_iota(jnp.int32, shape, len(shape) - 1)


def scan_lanes(growth, offset):
    lane = lane_index(growth.shape)
    stride = 1
    while stride < LANES:
        inside = lane >= stride
        lead_growth = pltpu.roll(growth, stride, 1)
        lead_offset = pltpu.roll(offset, stride, 1)
        offset = jnp.where(inside, growth * lead_offset + offset, offset)
        growth = jnp.where(inside, growth * lead_growth, growth)
        stride *= 2
    return growth, offset


def solve_block(courants, sources):
    out, end = [], None
    for courant, source in zip(courants, sources):
        above = 1.0 + courant
        shared = 1.0 / (courant * above)
        ratio = 1.0 - shared * courant
        inverse = shared * above
        growth, offset = scan_lanes(ratio, ratio * source)
        if end is not None:
            offset = growth * end[1] + offset
            growth = growth * end[0]
        end = (
            jnp.broadcast_to(growth[:, LANES - 1 :], growth.shape),
            jnp.broadcast_to(offset[:, LANES - 1 :], offset.shape),
        )
        out.append((growth * inverse, offset * inverse))
    return out, end


def kernel(
    n, z, tracer, courant, hops_in, area_in, updated, dateline,
    trv, cov, st, ct, gs, os, maps, pt, pc, pu, back, part,
    hops, area, small_sem, in_sem, own_sem, p_send, p_recv, m_send, m_recv, b_send, b_recv, d_send, d_recv,
):
    levels, rows, cells = trv.shape
    halves = cells // LANES
    me = lax.axis_index("lon")
    lat = lax.axis_index("lat")
    polar = (lat == 0) | (lat == z - 1)
    row0 = pl.multiple_of(jnp.where(lat == 0, 0, rows - POLAR), POLAR)
    slab = pl.ds(row0, POLAR)

    def ahead(k):
        return lax.rem(me + k, n)

    def behind(k):
        return lax.rem(me + n - k, n)

    def is_worker(device, work):
        if n == levels:
            work()
        else:
            pl.when(device < levels)(work)

    barrier = pltpu.get_barrier_semaphore()
    for k in range(1, n):
        pl.semaphore_signal(barrier, inc=1, device_id={"lon": ahead(k)}, device_id_type=pl.DeviceIdType.MESH)
    for k in range(1, z):
        pl.semaphore_signal(
            barrier, inc=1, device_id={"lat": lax.rem(lat + k, z)}, device_id_type=pl.DeviceIdType.MESH
        )

    def load(l):
        some = pl.ds(l, GROUP)
        return (
            pltpu.make_async_copy(tracer.at[some], trv.at[some], in_sem.at[0, l]),
            pltpu.make_async_copy(courant.at[some], cov.at[some], in_sem.at[1, l]),
        )

    for l in range(0, levels, GROUP):
        for copy in load(l):
            copy.start()
    small = (
        pltpu.make_async_copy(hops_in, hops, small_sem.at[0]),
        pltpu.make_async_copy(area_in, area, small_sem.at[1]),
    )
    for copy in small:
        copy.start()

    def remote(source, target, send, recv, k, axis="lon"):
        place = ahead(k) if axis == "lon" else lax.rem(lat + k, z)
        return pltpu.make_async_remote_copy(
            src_ref=source, dst_ref=target, send_sem=send, recv_sem=recv,
            device_id={axis: place}, device_id_type=pl.DeviceIdType.MESH,
        )

    def polar_out(k):
        level = lax.rem(ahead(k), levels)
        return (
            remote(courant.at[level, slab], pc.at[me], p_send.at[0, k], p_recv.at[0, k], k),
            remote(tracer.at[level, slab], pt.at[me], p_send.at[1, k], p_recv.at[1, k], k),
        )

    def polar_own():
        level = lax.rem(me, levels)
        return (
            pltpu.make_async_copy(courant.at[level, slab], pc.at[me], own_sem.at[0]),
            pltpu.make_async_copy(tracer.at[level, slab], pt.at[me], own_sem.at[1]),
        )

    pl.semaphore_wait(barrier, n + z - 2)

    @pl.when(polar)
    def _():
        for k in range(1, n):
            def send(k=k):
                for copy in polar_out(k):
                    copy.start()
            is_worker(ahead(k), send)

        def own():
            for copy in polar_own():
                copy.start()
        is_worker(me, own)

    steps = cells // CHUNKS

    def turn(l):
        for h in range(halves):
            c = pl.ds(h * LANES, LANES)
            here = cov[l, :, c]
            above = 1.0 + here
            shared = 1.0 / (here * above)
            ratio = 1.0 - shared * here
            cov[l, :, c] = shared * above
            ct[l, c, :] = jnp.transpose(ratio)
            st[l, c, :] = jnp.transpose(ratio * trv[l, :, c])

    def run(l):
        growth = offset = None
        for v in range(steps):
            cells_v = pl.ds(v, CHUNKS, stride=steps)
            ratio, source = ct[l, cells_v, :], st[l, cells_v, :]
            growth = ratio if v == 0 else growth * ratio
            offset = source if v == 0 else ratio * offset + source
            gs[l, v] = growth
            os[l, v] = offset
        return growth, offset

    growth, offset = [], []
    for l in range(levels + 1):
        if l < levels:
            if l % GROUP == 0:
                for copy in load(l):
                    copy.wait()
            turn(l)
        if l > 0:
            g, o = run(l - 1)
            growth.append(g)
            offset.append(o)
    for copy in small:
        copy.wait()
    sub = lax.broadcasted_iota(jnp.int32, (CHUNKS, rows), 0)
    before = []
    for l in range(levels):
        g, o = growth[l], offset[l]
        stride = 1
        while stride < CHUNKS:
            inside = sub >= stride
            lead_g, lead_o = pltpu.roll(g, stride, 0), pltpu.roll(o, stride, 0)
            o = jnp.where(inside, g * lead_o + o, o)
            g = jnp.where(inside, g * lead_g, g)
            stride *= 2
        maps[me, l : l + 1, :] = g[CHUNKS - 1 :]
        maps[me, levels + l : levels + l + 1, :] = o[CHUNKS - 1 :]
        before.append(
            (jnp.where(sub == 0, 1.0, pltpu.roll(g, 1, 0)), jnp.where(sub == 0, 0.0, pltpu.roll(o, 1, 0)))
        )

    def map_out(k):
        return remote(maps.at[me], maps.at[me], m_send.at[k], m_recv.at[k], k)

    for k in range(1, n):
        map_out(k).start()

    lane = lane_index((POLAR, LANES))
    sublane = lax.broadcasted_iota(jnp.int32, (POLAR, LANES), 0)

    def back_out(k):
        return remote(
            pu.at[ahead(k)], back.at[lax.rem(me, levels)], b_send.at[k], b_recv.at[k], k
        )

    def column(values):
        place = lane_index((POLAR, rows)) == lax.broadcasted_iota(jnp.int32, (POLAR, rows), 0) + row0
        return jnp.sum(jnp.where(place, jnp.broadcast_to(values, (POLAR, rows)), 0.0), axis=1, keepdims=True)

    def solve_polar():
        for k in range(1, n):
            for copy in polar_out(k):
                copy.wait_recv()
        for copy in polar_own():
            copy.wait()
        count = jnp.broadcast_to(column(hops[...].astype(jnp.float32)), (POLAR, LANES)).astype(jnp.int32)
        courants, sources = [], []
        for h in range(halves):
            c = pl.ds(h * LANES, LANES)
            blocks = [pt[s, :, c] for s in range(n)]
            for bit in range(STOPS.bit_length()):
                chosen = jnp.right_shift(count, bit) % 2 == 1
                blocks = [
                    jnp.where(chosen, blocks[(s - (1 << bit)) % n], blocks[s]) for s in range(n)
                ]
            sources.append(jnp.concatenate(blocks, axis=0))
            courants.append(jnp.concatenate([pc[s, :, c] for s in range(n)], axis=0))
        out, end = solve_block(courants, sources)
        growth = jnp.ones((POLAR, LANES), jnp.float32)
        offset = jnp.zeros((POLAR, LANES), jnp.float32)
        prior = []
        for s in range(n):
            prior.append((growth, offset))
            own = slice(s * POLAR, (s + 1) * POLAR)
            offset = end[0][own] * offset + end[1][own]
            growth = growth * end[0][own]
        wrap = offset / (1.0 - growth)
        weighted = jnp.sum(column(area[...]) * wrap, axis=0, keepdims=True)
        weighted = jnp.broadcast_to(weighted, (POLAR, LANES))
        for s in range(n):
            inflow = prior[s][0] * wrap + prior[s][1]
            own = slice(s * POLAR, (s + 1) * POLAR)
            for h, (g, o) in enumerate(out):
                c = pl.ds(h * LANES, LANES)
                pu[s, :POLAR, c] = g[own] * inflow + o[own]
                pu[s, POLAR:, c] = weighted
        for k in range(1, n):
            back_out(k).start()
        back[lax.rem(me, levels)] = pu[me]

    @pl.when(polar)
    def _():
        is_worker(me, solve_polar)

    for k in range(1, n):
        map_out(k).wait_recv()
    growth = jnp.ones((levels, rows), jnp.float32)
    offset = jnp.zeros((levels, rows), jnp.float32)
    prior_growth, prior_offset = growth, offset
    for s in range(n):
        here = s == me
        prior_growth = jnp.where(here, growth, prior_growth)
        prior_offset = jnp.where(here, offset, prior_offset)
        own = maps[s]
        offset = own[:levels] * offset + own[levels:]
        growth = growth * own[:levels]
    wrap = offset / (1.0 - growth)
    inflow = prior_growth * wrap + prior_offset
    areas = jnp.broadcast_to(area[...], (levels, rows))
    row = lane_index((levels, rows))
    masked = polar & (row >= row0) & (row < row0 + POLAR)
    part[lat, :levels] = jnp.where(masked, 0.0, areas * wrap)
    part[lat, levels:] = areas

    for l in range(levels):
        entry = before[l][0] * inflow[l : l + 1] + before[l][1]
        for v in range(steps):
            ct[l, pl.ds(v, CHUNKS, stride=steps), :] = gs[l, v] * entry + os[l, v]
        for h in range(halves):
            c = pl.ds(h * LANES, LANES)
            updated[l, :, c] = jnp.transpose(ct[l, c, :]) * cov[l, :, c]

    def part_out(k):
        return remote(part.at[lat], part.at[lat], d_send.at[k], d_recv.at[k], k, "lat")

    @pl.when(polar)
    def _():
        for k in range(1, n):
            def receive(k=k):
                back_out(k).wait_recv()
            is_worker(behind(k), receive)
        total = jnp.zeros((levels, LANES), jnp.float32)
        sub = lax.broadcasted_iota(jnp.int32, (levels, LANES), 0)
        for l in range(levels):
            total = jnp.where(sub == l, back[l, POLAR : POLAR + 1, :LANES], total)
        first_lane = lane_index((levels, LANES)) == 0
        part[lat, :levels, :LANES] = part[lat, :levels, :LANES] + jnp.where(first_lane, total, 0.0)

    for k in range(1, z):
        part_out(k).start()

    @pl.when(polar)
    def _():
        for l in range(levels):
            updated[l, slab, :] = back[l, :POLAR, :]

    for k in range(1, z):
        part_out(k).wait_recv()
    total = part[0]
    for s in range(1, z):
        total = total + part[s]
    sums = jnp.sum(total, axis=1, keepdims=True)
    mean = jnp.broadcast_to(sums[:levels] / sums[levels:], (levels, LANES))
    diagonal = lax.broadcasted_iota(jnp.int32, (levels, LANES), 0) == lane_index((levels, LANES))
    dateline[...] = jnp.sum(jnp.where(diagonal, mean, 0.0), axis=0, keepdims=True)[:, :levels]

    for k in range(1, z):
        part_out(k).wait_send()
    for k in range(1, n):
        map_out(k).wait_send()

    @pl.when(polar)
    def _():
        for k in range(1, n):
            def sent(k=k):
                for copy in polar_out(k):
                    copy.wait_send()
            is_worker(ahead(k), sent)

        def returned():
            for k in range(1, n):
                back_out(k).wait_send()
        is_worker(me, returned)


def write_out(updated_in, dateline_in, updated, dateline, sem):
    copies = (
        pltpu.make_async_copy(updated_in, updated, sem.at[0]),
        pltpu.make_async_copy(dateline_in, dateline, sem.at[1]),
    )
    for copy in copies:
        copy.start()
    for copy in copies:
        copy.wait()


def body(n, z, tracer, courant, hop_counts, row_area):
    levels, rows, cells = tracer.shape
    f32 = jnp.float32
    vmem = pl.BlockSpec(memory_space=pltpu.VMEM)
    hbm = pl.BlockSpec(memory_space=pl.ANY)
    dma = pltpu.SemaphoreType.DMA
    inputs = (tracer, courant, hop_counts.reshape(1, rows), row_area.reshape(1, rows))
    updated, dateline = pl.pallas_call(
        functools.partial(kernel, n, z),
        out_shape=(
            pltpu.VMEM(tracer.shape, f32),
            pltpu.VMEM((1, levels), f32),
        ),
        in_specs=[hbm] * 4,
        out_specs=(vmem, vmem),
        scratch_shapes=[
            pltpu.VMEM(tracer.shape, f32),
            pltpu.VMEM(tracer.shape, f32),
            pltpu.VMEM((levels, cells, rows), f32),
            pltpu.VMEM((levels, cells, rows), f32),
            pltpu.VMEM((levels, cells // CHUNKS, CHUNKS, rows), f32),
            pltpu.VMEM((levels, cells // CHUNKS, CHUNKS, rows), f32),
            pltpu.VMEM((n, 2 * levels, rows), f32),
            pltpu.VMEM((n, POLAR, cells), f32),
            pltpu.VMEM((n, POLAR, cells), f32),
            pltpu.VMEM((n, 2 * POLAR, cells), f32),
            pltpu.VMEM((levels, 2 * POLAR, cells), f32),
            pltpu.VMEM((z, 2 * levels, rows), f32),
            pltpu.VMEM((1, rows), jnp.int32),
            pltpu.VMEM((1, rows), f32),
            dma((2,)), dma((2, levels)), dma((2,)),
            dma((2, n)), dma((2, n)),
            dma((n,)), dma((n,)),
            dma((n,)), dma((n,)),
            dma((z,)), dma((z,)),
        ],
        compiler_params=pltpu.CompilerParams(
            collective_id=0, has_side_effects=True, vmem_limit_bytes=24 * 1024 * 1024
        ),
        cost_estimate=pl.CostEstimate(
            flops=60 * tracer.size, bytes_accessed=12 * tracer.size, transcendentals=tracer.size
        ),
    )(*(pltpu.with_memory_space_constraint(a, pltpu.HBM) for a in inputs))
    held = (pltpu.with_memory_space_constraint(a, pltpu.VMEM) for a in (updated, dateline))
    updated, dateline = pl.pallas_call(
        write_out,
        out_shape=(pltpu.HBM(tracer.shape, f32), pltpu.HBM((1, levels), f32)),
        in_specs=[hbm, hbm],
        out_specs=(hbm, hbm),
        scratch_shapes=[dma((2,))],
    )(*held)
    return updated, dateline.reshape(levels)


def solution(mesh):
    return jax.shard_map(
        functools.partial(body, mesh.shape["lon"], mesh.shape["lat"]),
        mesh=mesh,
        in_specs=(P(None, "lat", "lon"), P(None, "lat", "lon"), P("lat"), P("lat")),
        out_specs=(P(None, "lat", "lon"), P()),
        check_vma=False,
    )
```

```python
import functools

import jax
import jax.numpy as jnp
from jax import lax
from jax.experimental import pallas as pl
from jax.experimental.pallas import tpu as pltpu
from jax.sharding import PartitionSpec as P

POLAR = 8
STOPS = 7
LANES = 128
CHUNKS = 8
GROUP = 2


def lane_index(shape):
    return lax.broadcasted_iota(jnp.int32, shape, len(shape) - 1)


def scan_lanes(growth, offset):
    lane = lane_index(growth.shape)
    stride = 1
    while stride < LANES:
        inside = lane >= stride
        lead_growth = pltpu.roll(growth, stride, 1)
        lead_offset = pltpu.roll(offset, stride, 1)
        offset = jnp.where(inside, growth * lead_offset + offset, offset)
        growth = jnp.where(inside, growth * lead_growth, growth)
        stride *= 2
    return growth, offset


def solve_block(courants, sources):
    out, end = [], None
    for courant, source in zip(courants, sources):
        above = 1.0 + courant
        shared = 1.0 / (courant * above)
        ratio = 1.0 - shared * courant
        inverse = shared * above
        growth, offset = scan_lanes(ratio, ratio * source)
        if end is not None:
            offset = growth * end[1] + offset
            growth = growth * end[0]
        end = (
            jnp.broadcast_to(growth[:, LANES - 1 :], growth.shape),
            jnp.broadcast_to(offset[:, LANES - 1 :], offset.shape),
        )
        out.append((growth * inverse, offset * inverse))
    return out, end


def kernel(
    n, z, tracer, courant, hops_in, area_in, updated, dateline,
    trv, cov, st, ct, gs, os, bg, bo, entry, maps, slabs, pin, pu, back, part, hops, area,
    small_sem, in_sem, slab_sem, p_sem, m_sem, b_sem, d_sem,
):
    levels, rows, cells = trv.shape
    halves = cells // LANES
    steps = cells // CHUNKS
    me = lax.axis_index("lon")
    lat = lax.axis_index("lat")
    polar = (lat == 0) | (lat == z - 1)
    row0 = pl.multiple_of(jnp.where(lat == 0, 0, rows - POLAR), POLAR)
    slab = pl.ds(row0, POLAR)
    own_level = lax.rem(me, levels)
    every = n == levels
    peers = n - 1 if every else levels - jnp.where(me < levels, 1, 0)

    def ahead(k):
        return lax.rem(me + k, n)

    def is_worker(device, work):
        if every:
            work()
        else:
            pl.when(device < levels)(work)

    barrier = pltpu.get_barrier_semaphore()
    for k in range(1, n):
        pl.semaphore_signal(barrier, inc=1, device_id={"lon": ahead(k)}, device_id_type=pl.DeviceIdType.MESH)
    for k in range(1, z):
        pl.semaphore_signal(
            barrier, inc=1, device_id={"lat": lax.rem(lat + k, z)}, device_id_type=pl.DeviceIdType.MESH
        )

    def load_slabs():
        return (
            pltpu.make_async_copy(courant.at[:, slab], slabs.at[:, 0], slab_sem.at[0]),
            pltpu.make_async_copy(tracer.at[:, slab], slabs.at[:, 1], slab_sem.at[1]),
        )

    @pl.when(polar)
    def _():
        for copy in load_slabs():
            copy.start()

    def load(l):
        some = pl.ds(l, GROUP)
        return (
            pltpu.make_async_copy(tracer.at[some], trv.at[some], in_sem.at[0, l]),
            pltpu.make_async_copy(courant.at[some], cov.at[some], in_sem.at[1, l]),
        )

    for l in range(0, levels, GROUP):
        for copy in load(l):
            copy.start()
    small = (
        pltpu.make_async_copy(hops_in, hops, small_sem.at[0]),
        pltpu.make_async_copy(area_in, area, small_sem.at[1]),
    )
    for copy in small:
        copy.start()

    def send(source, target, sem, k, axis="lon"):
        place = ahead(k) if axis == "lon" else lax.rem(lat + k, z)
        pltpu.make_async_remote_copy(
            src_ref=source, dst_ref=target, send_sem=sem.at[0], recv_sem=sem.at[1],
            device_id={axis: place}, device_id_type=pl.DeviceIdType.MESH,
        ).start()

    def wait(slots, sem, count):
        if isinstance(count, int):
            some = slots.at[pl.ds(0, count)]
            pltpu.make_async_copy(some, some, sem).wait()
        else:
            @pl.loop(0, count)
            def _(_):
                pltpu.make_async_copy(slots.at[0], slots.at[0], sem).wait()

    pl.semaphore_wait(barrier, n + z - 2)

    @pl.when(polar)
    def _():
        for copy in load_slabs():
            copy.wait()
        for k in range(1, n):
            is_worker(ahead(k), lambda k=k: send(slabs.at[lax.rem(ahead(k), levels)], pin.at[me], p_sem, k))
        pin[me] = slabs[own_level]

    @pl.loop(0, levels, step=GROUP)
    def _(first):
        for copy in load(first):
            copy.wait()
        for l in range(GROUP):
            for h in range(halves):
                c = pl.ds(h * LANES, LANES)
                here = cov[first + l, :, c]
                above = 1.0 + here
                shared = 1.0 / (here * above)
                ratio = 1.0 - shared * here
                cov[first + l, :, c] = shared * above
                ct[first + l, c, :] = jnp.transpose(ratio)
                st[first + l, c, :] = jnp.transpose(ratio * trv[first + l, :, c])

    def step(v, state):
        growth, offset = state
        cells_v = pl.ds(v, CHUNKS, stride=steps)
        ratio = ct[:, cells_v, :]
        growth = growth * ratio
        offset = ratio * offset + st[:, cells_v, :]
        gs[v] = growth
        os[v] = offset
        return growth, offset

    shape = (levels, CHUNKS, rows)
    growth, offset = lax.fori_loop(
        0, steps, step, (jnp.ones(shape, jnp.float32), jnp.zeros(shape, jnp.float32)), unroll=4
    )
    for copy in small:
        copy.wait()
    sub = lax.broadcasted_iota(jnp.int32, (CHUNKS, rows), 0)
    for l in range(levels):
        g, o = growth[l], offset[l]
        stride = 1
        while stride < CHUNKS:
            inside = sub >= stride
            lead_g, lead_o = pltpu.roll(g, stride, 0), pltpu.roll(o, stride, 0)
            o = jnp.where(inside, g * lead_o + o, o)
            g = jnp.where(inside, g * lead_g, g)
            stride *= 2
        maps[me, l : l + 1, :] = g[CHUNKS - 1 :]
        maps[me, levels + l : levels + l + 1, :] = o[CHUNKS - 1 :]
        bg[l] = jnp.where(sub == 0, 1.0, pltpu.roll(g, 1, 0))
        bo[l] = jnp.where(sub == 0, 0.0, pltpu.roll(o, 1, 0))

    for k in range(1, n):
        send(maps.at[me], maps.at[me], m_sem, k)

    def column(values):
        place = lane_index((POLAR, rows)) == lax.broadcasted_iota(jnp.int32, (POLAR, rows), 0) + row0
        return jnp.sum(jnp.where(place, jnp.broadcast_to(values, (POLAR, rows)), 0.0), axis=1, keepdims=True)

    def solve_polar():
        count = jnp.broadcast_to(column(hops[...].astype(jnp.float32)), (POLAR, LANES)).astype(jnp.int32)
        weights = column(area[...])
        wait(pin, p_sem.at[1], n - 1)
        courants, sources = [], []
        for h in range(halves):
            c = pl.ds(h * LANES, LANES)
            blocks = [pin[s, 1, :, c] for s in range(n)]
            for bit in range(STOPS.bit_length()):
                chosen = jnp.right_shift(count, bit) % 2 == 1
                blocks = [
                    jnp.where(chosen, blocks[(s - (1 << bit)) % n], blocks[s]) for s in range(n)
                ]
            sources.append(jnp.concatenate(blocks, axis=0))
            courants.append(jnp.concatenate([pin[s, 0, :, c] for s in range(n)], axis=0))
        out, end = solve_block(courants, sources)
        growth = jnp.ones((POLAR, LANES), jnp.float32)
        offset = jnp.zeros((POLAR, LANES), jnp.float32)
        prior = []
        for s in range(n):
            prior.append((growth, offset))
            own = slice(s * POLAR, (s + 1) * POLAR)
            offset = end[0][own] * offset + end[1][own]
            growth = growth * end[0][own]
        wrap = offset / (1.0 - growth)
        weighted = jnp.broadcast_to(jnp.sum(weights * wrap, axis=0, keepdims=True), (POLAR, LANES))
        for s in range(n):
            inflow = prior[s][0] * wrap + prior[s][1]
            own = slice(s * POLAR, (s + 1) * POLAR)
            for h, (g, o) in enumerate(out):
                c = pl.ds(h * LANES, LANES)
                pu[s, :POLAR, c] = g[own] * inflow + o[own]
                pu[s, POLAR:, c] = weighted
        for k in range(1, n):
            send(pu.at[ahead(k)], back.at[own_level], b_sem, k)
        back[own_level] = pu[me]

    @pl.when(polar)
    def _():
        is_worker(me, solve_polar)

    wait(maps, m_sem.at[1], n - 1)
    growth = jnp.ones((levels, rows), jnp.float32)
    offset = jnp.zeros((levels, rows), jnp.float32)
    prior_growth, prior_offset = growth, offset
    for s in range(n):
        here = s == me
        prior_growth = jnp.where(here, growth, prior_growth)
        prior_offset = jnp.where(here, offset, prior_offset)
        own = maps[s]
        offset = own[:levels] * offset + own[levels:]
        growth = growth * own[:levels]
    wrap = offset / (1.0 - growth)
    entry[...] = prior_growth * wrap + prior_offset

    areas = jnp.broadcast_to(area[...], (levels, rows))
    row = lane_index((levels, rows))
    masked = polar & (row >= row0) & (row < row0 + POLAR)
    part[lat, :levels] = jnp.where(masked, 0.0, areas * wrap)
    part[lat, levels:] = areas

    def write(low, high):
        @pl.loop(low, high, step=GROUP)
        def _(first):
            for l in range(GROUP):
                flow = bg[first + l] * entry[pl.ds(first + l, 1), :] + bo[first + l]
                for v in range(steps):
                    ct[first + l, pl.ds(v, CHUNKS, stride=steps), :] = gs[v, first + l] * flow + os[v, first + l]
                for h in range(halves):
                    c = pl.ds(h * LANES, LANES)
                    updated[first + l, :, c] = jnp.transpose(ct[first + l, c, :]) * cov[first + l, :, c]

    middle = levels // 2
    write(0, middle)

    @pl.when(polar)
    def _():
        wait(back, b_sem.at[1], peers)
        total = jnp.zeros((levels, LANES), jnp.float32)
        sub = lax.broadcasted_iota(jnp.int32, (levels, LANES), 0)
        for l in range(levels):
            total = jnp.where(sub == l, back[l, POLAR : POLAR + 1, :LANES], total)
        first_lane = lane_index((levels, LANES)) == 0
        part[lat, :levels, :LANES] = part[lat, :levels, :LANES] + jnp.where(first_lane, total, 0.0)

    for k in range(1, z):
        send(part.at[lat], part.at[lat], d_sem, k, "lat")

    write(middle, levels)

    @pl.when(polar)
    def _():
        for l in range(levels):
            updated[l, slab, :] = back[l, :POLAR, :]
        wait(slabs, p_sem.at[0], peers)
        is_worker(me, lambda: wait(pu, b_sem.at[0], n - 1))

    wait(maps, m_sem.at[0], n - 1)
    wait(part, d_sem.at[0], z - 1)
    wait(part, d_sem.at[1], z - 1)
    total = part[0]
    for s in range(1, z):
        total = total + part[s]
    sums = jnp.sum(total, axis=1, keepdims=True)
    mean = jnp.broadcast_to(sums[:levels] / sums[levels:], (levels, LANES))
    diagonal = lax.broadcasted_iota(jnp.int32, (levels, LANES), 0) == lane_index((levels, LANES))
    dateline[...] = jnp.sum(jnp.where(diagonal, mean, 0.0), axis=0, keepdims=True)[:, :levels]


def write_out(updated_in, dateline_in, updated, dateline, sem):
    copies = (
        pltpu.make_async_copy(updated_in, updated, sem.at[0]),
        pltpu.make_async_copy(dateline_in, dateline, sem.at[1]),
    )
    for copy in copies:
        copy.start()
    for copy in copies:
        copy.wait()


def body(n, z, tracer, courant, hop_counts, row_area):
    levels, rows, cells = tracer.shape
    f32 = jnp.float32
    vmem = pl.BlockSpec(memory_space=pltpu.VMEM)
    hbm = pl.BlockSpec(memory_space=pl.ANY)
    dma = pltpu.SemaphoreType.DMA
    inputs = (tracer, courant, hop_counts.reshape(1, rows), row_area.reshape(1, rows))
    updated, dateline = pl.pallas_call(
        functools.partial(kernel, n, z),
        out_shape=(
            pltpu.VMEM(tracer.shape, f32),
            pltpu.VMEM((1, levels), f32),
        ),
        in_specs=[hbm] * 4,
        out_specs=(vmem, vmem),
        scratch_shapes=[
            pltpu.VMEM(tracer.shape, f32),
            pltpu.VMEM(tracer.shape, f32),
            pltpu.VMEM((levels, cells, rows), f32),
            pltpu.VMEM((levels, cells, rows), f32),
            pltpu.VMEM((cells // CHUNKS, levels, CHUNKS, rows), f32),
            pltpu.VMEM((cells // CHUNKS, levels, CHUNKS, rows), f32),
            pltpu.VMEM((levels, CHUNKS, rows), f32),
            pltpu.VMEM((levels, CHUNKS, rows), f32),
            pltpu.VMEM((levels, rows), f32),
            pltpu.VMEM((n, 2 * levels, rows), f32),
            pltpu.VMEM((levels, 2, POLAR, cells), f32),
            pltpu.VMEM((n, 2, POLAR, cells), f32),
            pltpu.VMEM((n, 2 * POLAR, cells), f32),
            pltpu.VMEM((levels, 2 * POLAR, cells), f32),
            pltpu.VMEM((z, 2 * levels, rows), f32),
            pltpu.VMEM((1, rows), jnp.int32),
            pltpu.VMEM((1, rows), f32),
            dma((2,)), dma((2, levels)), dma((2,)),
            dma((2,)), dma((2,)), dma((2,)), dma((2,)),
        ],
        compiler_params=pltpu.CompilerParams(
            collective_id=0, has_side_effects=True, vmem_limit_bytes=24 * 1024 * 1024
        ),
        cost_estimate=pl.CostEstimate(
            flops=60 * tracer.size, bytes_accessed=12 * tracer.size, transcendentals=tracer.size
        ),
    )(*(pltpu.with_memory_space_constraint(a, pltpu.HBM) for a in inputs))
    held = (pltpu.with_memory_space_constraint(a, pltpu.VMEM) for a in (updated, dateline))
    updated, dateline = pl.pallas_call(
        write_out,
        out_shape=(pltpu.HBM(tracer.shape, f32), pltpu.HBM((1, levels), f32)),
        in_specs=[hbm, hbm],
        out_specs=(hbm, hbm),
        scratch_shapes=[dma((2,))],
    )(*held)
    return updated, dateline.reshape(levels)


def solution(mesh):
    return jax.shard_map(
        functools.partial(body, mesh.shape["lon"], mesh.shape["lat"]),
        mesh=mesh,
        in_specs=(P(None, "lat", "lon"), P(None, "lat", "lon"), P("lat"), P("lat")),
        out_specs=(P(None, "lat", "lon"), P()),
        check_vma=False,
    )
```

```python
import functools

import jax
import jax.numpy as jnp
from jax import lax
from jax.experimental import pallas as pl
from jax.experimental.pallas import tpu as pltpu
from jax.sharding import PartitionSpec as P

POLAR = 8
STOPS = 7
LANES = 128
CHUNKS = 8
GROUP = 2


def lane_index(shape):
    return lax.broadcasted_iota(jnp.int32, shape, len(shape) - 1)


def scan_lanes(growth, offset):
    lane = lane_index(growth.shape)
    stride = 1
    while stride < LANES:
        inside = lane >= stride
        lead_growth = pltpu.roll(growth, stride, 1)
        lead_offset = pltpu.roll(offset, stride, 1)
        offset = jnp.where(inside, growth * lead_offset + offset, offset)
        growth = jnp.where(inside, growth * lead_growth, growth)
        stride *= 2
    return growth, offset


def solve_block(courants, sources):
    out, end = [], None
    for courant, source in zip(courants, sources):
        above = 1.0 + courant
        shared = 1.0 / (courant * above)
        ratio = 1.0 - shared * courant
        inverse = shared * above
        growth, offset = scan_lanes(ratio, ratio * source)
        if end is not None:
            offset = growth * end[1] + offset
            growth = growth * end[0]
        end = (
            jnp.broadcast_to(growth[:, LANES - 1 :], growth.shape),
            jnp.broadcast_to(offset[:, LANES - 1 :], offset.shape),
        )
        out.append((growth * inverse, offset * inverse))
    return out, end


def kernel(
    n, z, tracer, courant, hops_in, area_in, updated, dateline,
    trv, cov, st, ct, gs, os, bg, bo, entry, maps, slabs, pin, pu, back, part, hops, area,
    small_sem, in_sem, slab_sem, p_sem, m_sem, b_sem, d_sem,
):
    levels, rows, cells = trv.shape
    halves = cells // LANES
    steps = cells // CHUNKS
    me = lax.axis_index("lon")
    lat = lax.axis_index("lat")
    polar = (lat == 0) | (lat == z - 1)
    row0 = pl.multiple_of(jnp.where(lat == 0, 0, rows - POLAR), POLAR)
    slab = pl.ds(row0, POLAR)
    own_level = lax.rem(me, levels)
    every = n == levels
    peers = n - 1 if every else levels - jnp.where(me < levels, 1, 0)

    def ahead(k):
        return lax.rem(me + k, n)

    def is_worker(device, work):
        if every:
            work()
        else:
            pl.when(device < levels)(work)

    barrier = pltpu.get_barrier_semaphore()

    @pl.loop(1, n)
    def _(k):
        pl.semaphore_signal(barrier, inc=1, device_id={"lon": ahead(k)}, device_id_type=pl.DeviceIdType.MESH)

    @pl.loop(1, z)
    def _(k):
        pl.semaphore_signal(
            barrier, inc=1, device_id={"lat": lax.rem(lat + k, z)}, device_id_type=pl.DeviceIdType.MESH
        )

    def load_slabs():
        return (
            pltpu.make_async_copy(courant.at[:, slab], slabs.at[:, 0], slab_sem.at[0]),
            pltpu.make_async_copy(tracer.at[:, slab], slabs.at[:, 1], slab_sem.at[1]),
        )

    @pl.when(polar)
    def _():
        for copy in load_slabs():
            copy.start()

    def load(l):
        some = pl.ds(l, GROUP)
        return (
            pltpu.make_async_copy(tracer.at[some], trv.at[some], in_sem.at[0, l]),
            pltpu.make_async_copy(courant.at[some], cov.at[some], in_sem.at[1, l]),
        )

    for l in range(0, levels, GROUP):
        for copy in load(l):
            copy.start()
    small = (
        pltpu.make_async_copy(hops_in, hops, small_sem.at[0]),
        pltpu.make_async_copy(area_in, area, small_sem.at[1]),
    )
    for copy in small:
        copy.start()

    def send(source, target, sem, k, axis="lon"):
        place = ahead(k) if axis == "lon" else lax.rem(lat + k, z)
        pltpu.make_async_remote_copy(
            src_ref=source, dst_ref=target, send_sem=sem.at[0], recv_sem=sem.at[1],
            device_id={axis: place}, device_id_type=pl.DeviceIdType.MESH,
        ).start()

    def wait(slots, sem, count):
        if isinstance(count, int):
            some = slots.at[pl.ds(0, count)]
            pltpu.make_async_copy(some, some, sem).wait()
        else:
            @pl.loop(0, count)
            def _(_):
                pltpu.make_async_copy(slots.at[0], slots.at[0], sem).wait()

    pl.semaphore_wait(barrier, n + z - 2)

    @pl.when(polar)
    def _():
        for copy in load_slabs():
            copy.wait()

        @pl.loop(1, n)
        def _(k):
            is_worker(ahead(k), lambda: send(slabs.at[lax.rem(ahead(k), levels)], pin.at[me], p_sem, k))

        pin[me] = slabs[own_level]

    @pl.loop(0, levels, step=GROUP)
    def _(first):
        for copy in load(first):
            copy.wait()
        for l in range(GROUP):
            for h in range(halves):
                c = pl.ds(h * LANES, LANES)
                here = cov[first + l, :, c]
                above = 1.0 + here
                shared = 1.0 / (here * above)
                ratio = 1.0 - shared * here
                cov[first + l, :, c] = shared * above
                ct[first + l, c, :] = jnp.transpose(ratio)
                st[first + l, c, :] = jnp.transpose(ratio * trv[first + l, :, c])

    def step(v, state):
        growth, offset = state
        cells_v = pl.ds(v, CHUNKS, stride=steps)
        ratio = ct[:, cells_v, :]
        growth = growth * ratio
        offset = ratio * offset + st[:, cells_v, :]
        gs[v] = growth
        os[v] = offset
        return growth, offset

    shape = (levels, CHUNKS, rows)
    growth, offset = lax.fori_loop(
        0, steps, step, (jnp.ones(shape, jnp.float32), jnp.zeros(shape, jnp.float32)), unroll=4
    )
    for copy in small:
        copy.wait()
    sub = lax.broadcasted_iota(jnp.int32, (CHUNKS, rows), 0)
    for l in range(levels):
        g, o = growth[l], offset[l]
        stride = 1
        while stride < CHUNKS:
            inside = sub >= stride
            lead_g, lead_o = pltpu.roll(g, stride, 0), pltpu.roll(o, stride, 0)
            o = jnp.where(inside, g * lead_o + o, o)
            g = jnp.where(inside, g * lead_g, g)
            stride *= 2
        maps[me, l : l + 1, :] = g[CHUNKS - 1 :]
        maps[me, levels + l : levels + l + 1, :] = o[CHUNKS - 1 :]
        bg[l] = jnp.where(sub == 0, 1.0, pltpu.roll(g, 1, 0))
        bo[l] = jnp.where(sub == 0, 0.0, pltpu.roll(o, 1, 0))

    @pl.loop(1, n)
    def _(k):
        send(maps.at[me], maps.at[me], m_sem, k)

    def column(values):
        place = lane_index((POLAR, rows)) == lax.broadcasted_iota(jnp.int32, (POLAR, rows), 0) + row0
        return jnp.sum(jnp.where(place, jnp.broadcast_to(values, (POLAR, rows)), 0.0), axis=1, keepdims=True)

    def solve_polar():
        count = jnp.broadcast_to(column(hops[...].astype(jnp.float32)), (POLAR, LANES)).astype(jnp.int32)
        weights = column(area[...])
        wait(pin, p_sem.at[1], n - 1)
        courants, sources = [], []
        for h in range(halves):
            c = pl.ds(h * LANES, LANES)
            blocks = [pin[s, 1, :, c] for s in range(n)]
            for bit in range(STOPS.bit_length()):
                chosen = jnp.right_shift(count, bit) % 2 == 1
                blocks = [
                    jnp.where(chosen, blocks[(s - (1 << bit)) % n], blocks[s]) for s in range(n)
                ]
            sources.append(jnp.concatenate(blocks, axis=0))
            courants.append(jnp.concatenate([pin[s, 0, :, c] for s in range(n)], axis=0))
        out, end = solve_block(courants, sources)
        growth = jnp.ones((POLAR, LANES), jnp.float32)
        offset = jnp.zeros((POLAR, LANES), jnp.float32)
        prior = []
        for s in range(n):
            prior.append((growth, offset))
            own = slice(s * POLAR, (s + 1) * POLAR)
            offset = end[0][own] * offset + end[1][own]
            growth = growth * end[0][own]
        wrap = offset / (1.0 - growth)
        weighted = jnp.broadcast_to(jnp.sum(weights * wrap, axis=0, keepdims=True), (POLAR, LANES))
        for s in range(n):
            inflow = prior[s][0] * wrap + prior[s][1]
            own = slice(s * POLAR, (s + 1) * POLAR)
            for h, (g, o) in enumerate(out):
                c = pl.ds(h * LANES, LANES)
                pu[s, :POLAR, c] = g[own] * inflow + o[own]
                pu[s, POLAR:, c] = weighted

        @pl.loop(1, n)
        def _(k):
            send(pu.at[ahead(k)], back.at[own_level], b_sem, k)

        back[own_level] = pu[me]

    @pl.when(polar)
    def _():
        is_worker(me, solve_polar)

    wait(maps, m_sem.at[1], n - 1)
    growth = jnp.ones((levels, rows), jnp.float32)
    offset = jnp.zeros((levels, rows), jnp.float32)
    prior_growth, prior_offset = growth, offset
    for s in range(n):
        here = s == me
        prior_growth = jnp.where(here, growth, prior_growth)
        prior_offset = jnp.where(here, offset, prior_offset)
        own = maps[s]
        offset = own[:levels] * offset + own[levels:]
        growth = growth * own[:levels]
    wrap = offset / (1.0 - growth)
    entry[...] = prior_growth * wrap + prior_offset

    areas = jnp.broadcast_to(area[...], (levels, rows))
    row = lane_index((levels, rows))
    masked = polar & (row >= row0) & (row < row0 + POLAR)
    part[lat, :levels] = jnp.where(masked, 0.0, areas * wrap)
    part[lat, levels:] = areas

    def take_back():
        wait(back, b_sem.at[1], peers)
        total = jnp.zeros((levels, LANES), jnp.float32)
        sub = lax.broadcasted_iota(jnp.int32, (levels, LANES), 0)
        for l in range(levels):
            total = jnp.where(sub == l, back[l, POLAR : POLAR + 1, :LANES], total)
        first_lane = lane_index((levels, LANES)) == 0
        part[lat, :levels, :LANES] = part[lat, :levels, :LANES] + jnp.where(first_lane, total, 0.0)

    middle = levels // 2 // GROUP * GROUP

    @pl.loop(0, levels, step=GROUP)
    def _(first):
        @pl.when(first == middle)
        def _():
            pl.when(polar)(take_back)

            @pl.loop(1, z)
            def _(k):
                send(part.at[lat], part.at[lat], d_sem, k, "lat")

        for l in range(GROUP):
            flow = bg[first + l] * entry[pl.ds(first + l, 1), :] + bo[first + l]
            for v in range(steps):
                ct[first + l, pl.ds(v, CHUNKS, stride=steps), :] = gs[v, first + l] * flow + os[v, first + l]
            for h in range(halves):
                c = pl.ds(h * LANES, LANES)
                updated[first + l, :, c] = jnp.transpose(ct[first + l, c, :]) * cov[first + l, :, c]

    @pl.when(polar)
    def _():
        for l in range(levels):
            updated[l, slab, :] = back[l, :POLAR, :]
        wait(slabs, p_sem.at[0], peers)
        is_worker(me, lambda: wait(pu, b_sem.at[0], n - 1))

    wait(maps, m_sem.at[0], n - 1)
    wait(part, d_sem.at[0], z - 1)
    wait(part, d_sem.at[1], z - 1)
    total = part[0]
    for s in range(1, z):
        total = total + part[s]
    sums = jnp.sum(total, axis=1, keepdims=True)
    mean = jnp.broadcast_to(sums[:levels] / sums[levels:], (levels, LANES))
    diagonal = lax.broadcasted_iota(jnp.int32, (levels, LANES), 0) == lane_index((levels, LANES))
    dateline[...] = jnp.sum(jnp.where(diagonal, mean, 0.0), axis=0, keepdims=True)[:, :levels]


def write_out(updated_in, dateline_in, updated, dateline, sem):
    levels = updated.shape[0]
    copies = [pltpu.make_async_copy(updated_in.at[l], updated.at[l], sem.at[l]) for l in range(levels)]
    copies.append(pltpu.make_async_copy(dateline_in, dateline, sem.at[levels]))
    for copy in copies:
        copy.start()
    for copy in copies:
        copy.wait()


def body(n, z, tracer, courant, hop_counts, row_area):
    levels, rows, cells = tracer.shape
    f32 = jnp.float32
    vmem = pl.BlockSpec(memory_space=pltpu.VMEM)
    hbm = pl.BlockSpec(memory_space=pl.ANY)
    dma = pltpu.SemaphoreType.DMA
    inputs = (tracer, courant, hop_counts.reshape(1, rows), row_area.reshape(1, rows))
    updated, dateline = pl.pallas_call(
        functools.partial(kernel, n, z),
        out_shape=(
            pltpu.VMEM(tracer.shape, f32),
            pltpu.VMEM((1, levels), f32),
        ),
        in_specs=[hbm] * 4,
        out_specs=(vmem, vmem),
        scratch_shapes=[
            pltpu.VMEM(tracer.shape, f32),
            pltpu.VMEM(tracer.shape, f32),
            pltpu.VMEM((levels, cells, rows), f32),
            pltpu.VMEM((levels, cells, rows), f32),
            pltpu.VMEM((cells // CHUNKS, levels, CHUNKS, rows), f32),
            pltpu.VMEM((cells // CHUNKS, levels, CHUNKS, rows), f32),
            pltpu.VMEM((levels, CHUNKS, rows), f32),
            pltpu.VMEM((levels, CHUNKS, rows), f32),
            pltpu.VMEM((levels, rows), f32),
            pltpu.VMEM((n, 2 * levels, rows), f32),
            pltpu.VMEM((levels, 2, POLAR, cells), f32),
            pltpu.VMEM((n, 2, POLAR, cells), f32),
            pltpu.VMEM((n, 2 * POLAR, cells), f32),
            pltpu.VMEM((levels, 2 * POLAR, cells), f32),
            pltpu.VMEM((z, 2 * levels, rows), f32),
            pltpu.VMEM((1, rows), jnp.int32),
            pltpu.VMEM((1, rows), f32),
            dma((2,)), dma((2, levels)), dma((2,)),
            dma((2,)), dma((2,)), dma((2,)), dma((2,)),
        ],
        compiler_params=pltpu.CompilerParams(
            collective_id=0, has_side_effects=True, vmem_limit_bytes=24 * 1024 * 1024
        ),
        cost_estimate=pl.CostEstimate(
            flops=60 * tracer.size, bytes_accessed=12 * tracer.size, transcendentals=tracer.size
        ),
    )(*(pltpu.with_memory_space_constraint(a, pltpu.HBM) for a in inputs))
    held = (pltpu.with_memory_space_constraint(a, pltpu.VMEM) for a in (updated, dateline))
    updated, dateline = pl.pallas_call(
        write_out,
        out_shape=(pltpu.HBM(tracer.shape, f32), pltpu.HBM((1, levels), f32)),
        in_specs=[hbm, hbm],
        out_specs=(hbm, hbm),
        scratch_shapes=[dma((levels + 1,))],
    )(*held)
    return updated, dateline.reshape(levels)


def solution(mesh):
    return jax.shard_map(
        functools.partial(body, mesh.shape["lon"], mesh.shape["lat"]),
        mesh=mesh,
        in_specs=(P(None, "lat", "lon"), P(None, "lat", "lon"), P("lat"), P("lat")),
        out_specs=(P(None, "lat", "lon"), P()),
        check_vma=False,
    )
```

```python
import functools

import jax
import jax.numpy as jnp
from jax import lax
from jax.experimental import pallas as pl
from jax.experimental.pallas import tpu as pltpu
from jax.sharding import PartitionSpec as P

POLAR = 8
STOPS = 7
LANES = 128
CHUNKS = 8
GROUP = 2
EARLY = 4


def lane_index(shape):
    return lax.broadcasted_iota(jnp.int32, shape, len(shape) - 1)


def scan_lanes(growth, offset):
    lane = lane_index(growth.shape)
    stride = 1
    while stride < LANES:
        inside = lane >= stride
        lead_growth = pltpu.roll(growth, stride, 1)
        lead_offset = pltpu.roll(offset, stride, 1)
        offset = jnp.where(inside, growth * lead_offset + offset, offset)
        growth = jnp.where(inside, growth * lead_growth, growth)
        stride *= 2
    return growth, offset


def solve_block(courants, sources):
    out, end = [], None
    for courant, source in zip(courants, sources):
        above = 1.0 + courant
        shared = 1.0 / (courant * above)
        ratio = 1.0 - shared * courant
        inverse = shared * above
        growth, offset = scan_lanes(ratio, ratio * source)
        if end is not None:
            offset = growth * end[1] + offset
            growth = growth * end[0]
        end = (
            jnp.broadcast_to(growth[:, LANES - 1 :], growth.shape),
            jnp.broadcast_to(offset[:, LANES - 1 :], offset.shape),
        )
        out.append((growth * inverse, offset * inverse))
    return out, end


def kernel(
    n, z, tracer, courant, hops_in, area_in, updated, dateline,
    trv, cov, st, ct, gs, os, bg, bo, entry, maps, slabs, pin, pu, back, part, hops, area,
    small_sem, in_sem, slab_sem, p_sem, m_sem, b_sem, d_sem,
):
    levels, rows, cells = trv.shape
    halves = cells // LANES
    steps = cells // CHUNKS
    me = lax.axis_index("lon")
    lat = lax.axis_index("lat")
    polar = (lat == 0) | (lat == z - 1)
    row0 = pl.multiple_of(jnp.where(lat == 0, 0, rows - POLAR), POLAR)
    slab = pl.ds(row0, POLAR)
    own_level = lax.rem(me, levels)
    every = n == levels
    peers = n - 1 if every else levels - jnp.where(me < levels, 1, 0)

    def ahead(k):
        return lax.rem(me + k, n)

    def is_worker(device, work):
        if every:
            work()
        else:
            pl.when(device < levels)(work)

    barrier = pltpu.get_barrier_semaphore()

    @pl.loop(1, n)
    def _(k):
        pl.semaphore_signal(barrier, inc=1, device_id={"lon": ahead(k)}, device_id_type=pl.DeviceIdType.MESH)

    @pl.loop(1, z)
    def _(k):
        pl.semaphore_signal(
            barrier, inc=1, device_id={"lat": lax.rem(lat + k, z)}, device_id_type=pl.DeviceIdType.MESH
        )

    def load_slabs():
        return (
            pltpu.make_async_copy(courant.at[:, slab], slabs.at[:, 0], slab_sem.at[0]),
            pltpu.make_async_copy(tracer.at[:, slab], slabs.at[:, 1], slab_sem.at[1]),
        )

    @pl.when(polar)
    def _():
        for copy in load_slabs():
            copy.start()

    def load(l):
        some = pl.ds(l, GROUP)
        return (
            pltpu.make_async_copy(tracer.at[some], trv.at[some], in_sem.at[0, l]),
            pltpu.make_async_copy(courant.at[some], cov.at[some], in_sem.at[1, l]),
        )

    for l in range(0, levels, GROUP):
        for copy in load(l):
            copy.start()
    small = (
        pltpu.make_async_copy(hops_in, hops, small_sem.at[0]),
        pltpu.make_async_copy(area_in, area, small_sem.at[1]),
    )
    for copy in small:
        copy.start()

    def send(source, target, sem, k, axis="lon"):
        place = ahead(k) if axis == "lon" else lax.rem(lat + k, z)
        pltpu.make_async_remote_copy(
            src_ref=source, dst_ref=target, send_sem=sem.at[0], recv_sem=sem.at[1],
            device_id={axis: place}, device_id_type=pl.DeviceIdType.MESH,
        ).start()

    def wait(slots, sem, count):
        if isinstance(count, int):
            some = slots.at[pl.ds(0, count)]
            pltpu.make_async_copy(some, some, sem).wait()
        else:
            @pl.loop(0, count)
            def _(_):
                pltpu.make_async_copy(slots.at[0], slots.at[0], sem).wait()

    def turn(first):
        for copy in load(first):
            copy.wait()
        for l in range(GROUP):
            for h in range(halves):
                c = pl.ds(h * LANES, LANES)
                here = cov[first + l, :, c]
                above = 1.0 + here
                shared = 1.0 / (here * above)
                ratio = 1.0 - shared * here
                cov[first + l, :, c] = shared * above
                ct[first + l, c, :] = jnp.transpose(ratio)
                st[first + l, c, :] = jnp.transpose(ratio * trv[first + l, :, c])

    early = levels * EARLY // 8 // GROUP * GROUP
    pl.loop(0, early, step=GROUP)(turn)

    pl.semaphore_wait(barrier, n + z - 2)

    @pl.when(polar)
    def _():
        for copy in load_slabs():
            copy.wait()

        @pl.loop(1, n)
        def _(k):
            is_worker(ahead(k), lambda: send(slabs.at[lax.rem(ahead(k), levels)], pin.at[me], p_sem, k))

        pin[me] = slabs[own_level]

    pl.loop(early, levels, step=GROUP)(turn)

    def step(v, state):
        growth, offset = state
        cells_v = pl.ds(v, CHUNKS, stride=steps)
        ratio = ct[:, cells_v, :]
        growth = growth * ratio
        offset = ratio * offset + st[:, cells_v, :]
        gs[v] = growth
        os[v] = offset
        return growth, offset

    shape = (levels, CHUNKS, rows)
    growth, offset = lax.fori_loop(
        0, steps, step, (jnp.ones(shape, jnp.float32), jnp.zeros(shape, jnp.float32)), unroll=4
    )
    for copy in small:
        copy.wait()
    sub = lax.broadcasted_iota(jnp.int32, (CHUNKS, rows), 0)
    for l in range(levels):
        g, o = growth[l], offset[l]
        stride = 1
        while stride < CHUNKS:
            inside = sub >= stride
            lead_g, lead_o = pltpu.roll(g, stride, 0), pltpu.roll(o, stride, 0)
            o = jnp.where(inside, g * lead_o + o, o)
            g = jnp.where(inside, g * lead_g, g)
            stride *= 2
        maps[me, l : l + 1, :] = g[CHUNKS - 1 :]
        maps[me, levels + l : levels + l + 1, :] = o[CHUNKS - 1 :]
        bg[l] = jnp.where(sub == 0, 1.0, pltpu.roll(g, 1, 0))
        bo[l] = jnp.where(sub == 0, 0.0, pltpu.roll(o, 1, 0))

    @pl.loop(1, n)
    def _(k):
        send(maps.at[me], maps.at[me], m_sem, k)

    def column(values):
        place = lane_index((POLAR, rows)) == lax.broadcasted_iota(jnp.int32, (POLAR, rows), 0) + row0
        return jnp.sum(jnp.where(place, jnp.broadcast_to(values, (POLAR, rows)), 0.0), axis=1, keepdims=True)

    def solve_polar():
        count = jnp.broadcast_to(column(hops[...].astype(jnp.float32)), (POLAR, LANES)).astype(jnp.int32)
        weights = column(area[...])
        wait(pin, p_sem.at[1], n - 1)
        courants, sources = [], []
        for h in range(halves):
            c = pl.ds(h * LANES, LANES)
            blocks = [pin[s, 1, :, c] for s in range(n)]
            for bit in range(STOPS.bit_length()):
                chosen = jnp.right_shift(count, bit) % 2 == 1
                blocks = [
                    jnp.where(chosen, blocks[(s - (1 << bit)) % n], blocks[s]) for s in range(n)
                ]
            sources.append(jnp.concatenate(blocks, axis=0))
            courants.append(jnp.concatenate([pin[s, 0, :, c] for s in range(n)], axis=0))
        out, end = solve_block(courants, sources)
        growth = jnp.ones((POLAR, LANES), jnp.float32)
        offset = jnp.zeros((POLAR, LANES), jnp.float32)
        prior = []
        for s in range(n):
            prior.append((growth, offset))
            own = slice(s * POLAR, (s + 1) * POLAR)
            offset = end[0][own] * offset + end[1][own]
            growth = growth * end[0][own]
        wrap = offset / (1.0 - growth)
        weighted = jnp.broadcast_to(jnp.sum(weights * wrap, axis=0, keepdims=True), (POLAR, LANES))
        for s in range(n):
            inflow = prior[s][0] * wrap + prior[s][1]
            own = slice(s * POLAR, (s + 1) * POLAR)
            for h, (g, o) in enumerate(out):
                c = pl.ds(h * LANES, LANES)
                pu[s, :POLAR, c] = g[own] * inflow + o[own]
                pu[s, POLAR:, c] = weighted

        @pl.loop(1, n)
        def _(k):
            send(pu.at[ahead(k)], back.at[own_level], b_sem, k)

        back[own_level] = pu[me]

    @pl.when(polar)
    def _():
        is_worker(me, solve_polar)

    wait(maps, m_sem.at[1], n - 1)
    growth = jnp.ones((levels, rows), jnp.float32)
    offset = jnp.zeros((levels, rows), jnp.float32)
    prior_growth, prior_offset = growth, offset
    for s in range(n):
        here = s == me
        prior_growth = jnp.where(here, growth, prior_growth)
        prior_offset = jnp.where(here, offset, prior_offset)
        own = maps[s]
        offset = own[:levels] * offset + own[levels:]
        growth = growth * own[:levels]
    wrap = offset / (1.0 - growth)
    entry[...] = prior_growth * wrap + prior_offset

    areas = jnp.broadcast_to(area[...], (levels, rows))
    row = lane_index((levels, rows))
    masked = polar & (row >= row0) & (row < row0 + POLAR)
    part[lat, :levels] = jnp.where(masked, 0.0, areas * wrap)
    part[lat, levels:] = areas

    def take_back():
        wait(back, b_sem.at[1], peers)
        total = jnp.zeros((levels, LANES), jnp.float32)
        sub = lax.broadcasted_iota(jnp.int32, (levels, LANES), 0)
        for l in range(levels):
            total = jnp.where(sub == l, back[l, POLAR : POLAR + 1, :LANES], total)
        first_lane = lane_index((levels, LANES)) == 0
        part[lat, :levels, :LANES] = part[lat, :levels, :LANES] + jnp.where(first_lane, total, 0.0)

    middle = levels // 2 // GROUP * GROUP

    @pl.loop(0, levels, step=GROUP)
    def _(first):
        @pl.when(first == middle)
        def _():
            pl.when(polar)(take_back)

            @pl.loop(1, z)
            def _(k):
                send(part.at[lat], part.at[lat], d_sem, k, "lat")

        for l in range(GROUP):
            flow = bg[first + l] * entry[pl.ds(first + l, 1), :] + bo[first + l]
            for v in range(steps):
                ct[first + l, pl.ds(v, CHUNKS, stride=steps), :] = gs[v, first + l] * flow + os[v, first + l]
            for h in range(halves):
                c = pl.ds(h * LANES, LANES)
                updated[first + l, :, c] = jnp.transpose(ct[first + l, c, :]) * cov[first + l, :, c]

    @pl.when(polar)
    def _():
        for l in range(levels):
            updated[l, slab, :] = back[l, :POLAR, :]
        wait(slabs, p_sem.at[0], peers)
        is_worker(me, lambda: wait(pu, b_sem.at[0], n - 1))

    wait(maps, m_sem.at[0], n - 1)
    wait(part, d_sem.at[0], z - 1)
    wait(part, d_sem.at[1], z - 1)
    total = part[0]
    for s in range(1, z):
        total = total + part[s]
    sums = jnp.sum(total, axis=1, keepdims=True)
    mean = jnp.broadcast_to(sums[:levels] / sums[levels:], (levels, LANES))
    diagonal = lax.broadcasted_iota(jnp.int32, (levels, LANES), 0) == lane_index((levels, LANES))
    dateline[...] = jnp.sum(jnp.where(diagonal, mean, 0.0), axis=0, keepdims=True)[:, :levels]


def write_out(updated_in, dateline_in, updated, dateline, sem):
    copies = (
        pltpu.make_async_copy(updated_in, updated, sem.at[0]),
        pltpu.make_async_copy(dateline_in, dateline, sem.at[1]),
    )
    for copy in copies:
        copy.start()
    for copy in copies:
        copy.wait()


def body(n, z, tracer, courant, hop_counts, row_area):
    levels, rows, cells = tracer.shape
    f32 = jnp.float32
    vmem = pl.BlockSpec(memory_space=pltpu.VMEM)
    hbm = pl.BlockSpec(memory_space=pl.ANY)
    dma = pltpu.SemaphoreType.DMA
    inputs = (tracer, courant, hop_counts.reshape(1, rows), row_area.reshape(1, rows))
    updated, dateline = pl.pallas_call(
        functools.partial(kernel, n, z),
        out_shape=(
            pltpu.VMEM(tracer.shape, f32),
            pltpu.VMEM((1, levels), f32),
        ),
        in_specs=[hbm] * 4,
        out_specs=(vmem, vmem),
        scratch_shapes=[
            pltpu.VMEM(tracer.shape, f32),
            pltpu.VMEM(tracer.shape, f32),
            pltpu.VMEM((levels, cells, rows), f32),
            pltpu.VMEM((levels, cells, rows), f32),
            pltpu.VMEM((cells // CHUNKS, levels, CHUNKS, rows), f32),
            pltpu.VMEM((cells // CHUNKS, levels, CHUNKS, rows), f32),
            pltpu.VMEM((levels, CHUNKS, rows), f32),
            pltpu.VMEM((levels, CHUNKS, rows), f32),
            pltpu.VMEM((levels, rows), f32),
            pltpu.VMEM((n, 2 * levels, rows), f32),
            pltpu.VMEM((levels, 2, POLAR, cells), f32),
            pltpu.VMEM((n, 2, POLAR, cells), f32),
            pltpu.VMEM((n, 2 * POLAR, cells), f32),
            pltpu.VMEM((levels, 2 * POLAR, cells), f32),
            pltpu.VMEM((z, 2 * levels, rows), f32),
            pltpu.VMEM((1, rows), jnp.int32),
            pltpu.VMEM((1, rows), f32),
            dma((2,)), dma((2, levels)), dma((2,)),
            dma((2,)), dma((2,)), dma((2,)), dma((2,)),
        ],
        compiler_params=pltpu.CompilerParams(
            collective_id=0, has_side_effects=True, vmem_limit_bytes=24 * 1024 * 1024
        ),
        cost_estimate=pl.CostEstimate(
            flops=60 * tracer.size, bytes_accessed=12 * tracer.size, transcendentals=tracer.size
        ),
    )(*(pltpu.with_memory_space_constraint(a, pltpu.HBM) for a in inputs))
    held = (pltpu.with_memory_space_constraint(a, pltpu.VMEM) for a in (updated, dateline))
    updated, dateline = pl.pallas_call(
        write_out,
        out_shape=(pltpu.HBM(tracer.shape, f32), pltpu.HBM((1, levels), f32)),
        in_specs=[hbm, hbm],
        out_specs=(hbm, hbm),
        scratch_shapes=[dma((2,))],
    )(*held)
    return updated, dateline.reshape(levels)


def solution(mesh):
    return jax.shard_map(
        functools.partial(body, mesh.shape["lon"], mesh.shape["lat"]),
        mesh=mesh,
        in_specs=(P(None, "lat", "lon"), P(None, "lat", "lon"), P("lat"), P("lat")),
        out_specs=(P(None, "lat", "lon"), P()),
        check_vma=False,
    )
```

```python
import functools

import jax
import jax.numpy as jnp
from jax import lax
from jax.experimental import pallas as pl
from jax.experimental.pallas import tpu as pltpu
from jax.sharding import PartitionSpec as P

POLAR = 8
STOPS = 7
LANES = 128
CHUNKS = 8
GROUP = 2
EARLY = 4


def lane_index(shape):
    return lax.broadcasted_iota(jnp.int32, shape, len(shape) - 1)


def scan_lanes(growth, offset):
    lane = lane_index(growth.shape)
    stride = 1
    while stride < LANES:
        inside = lane >= stride
        lead_growth = pltpu.roll(growth, stride, 1)
        lead_offset = pltpu.roll(offset, stride, 1)
        offset = jnp.where(inside, growth * lead_offset + offset, offset)
        growth = jnp.where(inside, growth * lead_growth, growth)
        stride *= 2
    return growth, offset


def solve_block(courants, sources):
    out, end = [], None
    for courant, source in zip(courants, sources):
        above = 1.0 + courant
        shared = 1.0 / (courant * above)
        ratio = 1.0 - shared * courant
        inverse = shared * above
        growth, offset = scan_lanes(ratio, ratio * source)
        if end is not None:
            offset = growth * end[1] + offset
            growth = growth * end[0]
        end = (
            jnp.broadcast_to(growth[:, LANES - 1 :], growth.shape),
            jnp.broadcast_to(offset[:, LANES - 1 :], offset.shape),
        )
        out.append((growth * inverse, offset * inverse))
    return out, end


def kernel(
    n, z, tracer, courant, hops_in, area_in, updated, dateline,
    trv, cov, order, st, ct, gs, os, bg, bo, entry, maps, slabs, pin, pu, back, part, hops, area,
    small_sem, in_sem, slab_sem, p_sem, m_sem, b_sem, d_sem,
):
    levels, rows, cells = trv.shape
    halves = cells // LANES
    steps = cells // CHUNKS
    me = lax.axis_index("lon")
    lat = lax.axis_index("lat")
    polar = (lat == 0) | (lat == z - 1)
    row0 = pl.multiple_of(jnp.where(lat == 0, 0, rows - POLAR), POLAR)
    slab = pl.ds(row0, POLAR)
    own_level = lax.rem(me, levels)
    every = n == levels
    peers = n - 1 if every else levels - jnp.where(me < levels, 1, 0)

    def ahead(k):
        return lax.rem(me + k, n)

    def is_worker(device, work):
        if every:
            work()
        else:
            pl.when(device < levels)(work)

    barrier = pltpu.get_barrier_semaphore()

    @pl.loop(1, n)
    def _(k):
        pl.semaphore_signal(barrier, inc=1, device_id={"lon": ahead(k)}, device_id_type=pl.DeviceIdType.MESH)

    @pl.loop(1, z)
    def _(k):
        pl.semaphore_signal(
            barrier, inc=1, device_id={"lat": lax.rem(lat + k, z)}, device_id_type=pl.DeviceIdType.MESH
        )

    def load_slabs():
        return (
            pltpu.make_async_copy(courant.at[:, slab], slabs.at[:, 0], slab_sem.at[0]),
            pltpu.make_async_copy(tracer.at[:, slab], slabs.at[:, 1], slab_sem.at[1]),
        )

    @pl.when(polar)
    def _():
        for copy in load_slabs():
            copy.start()

    def load(l):
        some = pl.ds(l, GROUP)
        return (
            pltpu.make_async_copy(tracer.at[some], trv.at[some], in_sem.at[0, l]),
            pltpu.make_async_copy(courant.at[some], cov.at[some], in_sem.at[1, l]),
        )

    for l in range(0, levels, GROUP):
        for copy in load(l):
            copy.start()
    small = (
        pltpu.make_async_copy(hops_in, hops, small_sem.at[0]),
        pltpu.make_async_copy(area_in, area, small_sem.at[1]),
    )
    for copy in small:
        copy.start()

    def send(source, target, sem, k, axis="lon"):
        place = ahead(k) if axis == "lon" else lax.rem(lat + k, z)
        pltpu.make_async_remote_copy(
            src_ref=source, dst_ref=target, send_sem=sem.at[0], recv_sem=sem.at[1],
            device_id={axis: place}, device_id_type=pl.DeviceIdType.MESH,
        ).start()

    def wait(slots, sem, count):
        if isinstance(count, int):
            some = slots.at[pl.ds(0, count)]
            pltpu.make_async_copy(some, some, sem).wait()
        else:
            @pl.loop(0, count)
            def _(_):
                pltpu.make_async_copy(slots.at[0], slots.at[0], sem).wait()

    place = lax.broadcasted_iota(jnp.int32, (cells, cells), 0)
    target = (place % CHUNKS) * steps + place // CHUNKS
    order[...] = jnp.where(lane_index((cells, cells)) == target, 1.0, 0.0).astype(jnp.bfloat16)

    def reorder(values):
        parts = []
        for _ in range(3):
            parts.append(values.astype(jnp.bfloat16))
            values = values - parts[-1].astype(jnp.float32)
        return lax.dot_general(
            jnp.concatenate([order[...]] * 3, axis=1), jnp.concatenate(parts, axis=1),
            (((1,), (1,)), ((), ())), preferred_element_type=jnp.float32,
        )

    def turn(first):
        for copy in load(first):
            copy.wait()
        for l in range(GROUP):
            here = cov[first + l]
            above = 1.0 + here
            shared = 1.0 / (here * above)
            ratio = 1.0 - shared * here
            cov[first + l] = shared * above
            both = reorder(jnp.concatenate([ratio, ratio * trv[first + l]], axis=0))
            ct[first + l] = both[:, :rows]
            st[first + l] = both[:, rows:]

    early = levels * EARLY // 8 // GROUP * GROUP
    pl.loop(0, early, step=GROUP)(turn)

    pl.semaphore_wait(barrier, n + z - 2)

    @pl.when(polar)
    def _():
        for copy in load_slabs():
            copy.wait()

        @pl.loop(1, n)
        def _(k):
            is_worker(ahead(k), lambda: send(slabs.at[lax.rem(ahead(k), levels)], pin.at[me], p_sem, k))

        pin[me] = slabs[own_level]

    pl.loop(early, levels, step=GROUP)(turn)

    def step(v, state):
        growth, offset = state
        cells_v = pl.ds(pl.multiple_of(v * CHUNKS, CHUNKS), CHUNKS)
        ratio = ct[:, cells_v, :]
        growth = growth * ratio
        offset = ratio * offset + st[:, cells_v, :]
        gs[v] = growth
        os[v] = offset
        return growth, offset

    shape = (levels, CHUNKS, rows)
    growth, offset = lax.fori_loop(
        0, steps, step, (jnp.ones(shape, jnp.float32), jnp.zeros(shape, jnp.float32)), unroll=4
    )
    for copy in small:
        copy.wait()
    sub = lax.broadcasted_iota(jnp.int32, (CHUNKS, rows), 0)
    for l in range(levels):
        g, o = growth[l], offset[l]
        stride = 1
        while stride < CHUNKS:
            inside = sub >= stride
            lead_g, lead_o = pltpu.roll(g, stride, 0), pltpu.roll(o, stride, 0)
            o = jnp.where(inside, g * lead_o + o, o)
            g = jnp.where(inside, g * lead_g, g)
            stride *= 2
        maps[me, l : l + 1, :] = g[CHUNKS - 1 :]
        maps[me, levels + l : levels + l + 1, :] = o[CHUNKS - 1 :]
        bg[l] = jnp.where(sub == 0, 1.0, pltpu.roll(g, 1, 0))
        bo[l] = jnp.where(sub == 0, 0.0, pltpu.roll(o, 1, 0))

    @pl.loop(1, n)
    def _(k):
        send(maps.at[me], maps.at[me], m_sem, k)

    def column(values):
        place = lane_index((POLAR, rows)) == lax.broadcasted_iota(jnp.int32, (POLAR, rows), 0) + row0
        return jnp.sum(jnp.where(place, jnp.broadcast_to(values, (POLAR, rows)), 0.0), axis=1, keepdims=True)

    def solve_polar():
        count = jnp.broadcast_to(column(hops[...].astype(jnp.float32)), (POLAR, LANES)).astype(jnp.int32)
        weights = column(area[...])
        wait(pin, p_sem.at[1], n - 1)
        courants, sources = [], []
        for h in range(halves):
            c = pl.ds(h * LANES, LANES)
            blocks = [pin[s, 1, :, c] for s in range(n)]
            for bit in range(STOPS.bit_length()):
                chosen = jnp.right_shift(count, bit) % 2 == 1
                blocks = [
                    jnp.where(chosen, blocks[(s - (1 << bit)) % n], blocks[s]) for s in range(n)
                ]
            sources.append(jnp.concatenate(blocks, axis=0))
            courants.append(jnp.concatenate([pin[s, 0, :, c] for s in range(n)], axis=0))
        out, end = solve_block(courants, sources)
        growth = jnp.ones((POLAR, LANES), jnp.float32)
        offset = jnp.zeros((POLAR, LANES), jnp.float32)
        prior = []
        for s in range(n):
            prior.append((growth, offset))
            own = slice(s * POLAR, (s + 1) * POLAR)
            offset = end[0][own] * offset + end[1][own]
            growth = growth * end[0][own]
        wrap = offset / (1.0 - growth)
        weighted = jnp.broadcast_to(jnp.sum(weights * wrap, axis=0, keepdims=True), (POLAR, LANES))
        for s in range(n):
            inflow = prior[s][0] * wrap + prior[s][1]
            own = slice(s * POLAR, (s + 1) * POLAR)
            for h, (g, o) in enumerate(out):
                c = pl.ds(h * LANES, LANES)
                pu[s, :POLAR, c] = g[own] * inflow + o[own]
                pu[s, POLAR:, c] = weighted

        @pl.loop(1, n)
        def _(k):
            send(pu.at[ahead(k)], back.at[own_level], b_sem, k)

        back[own_level] = pu[me]

    @pl.when(polar)
    def _():
        is_worker(me, solve_polar)

    wait(maps, m_sem.at[1], n - 1)
    growth = jnp.ones((levels, rows), jnp.float32)
    offset = jnp.zeros((levels, rows), jnp.float32)
    prior_growth, prior_offset = growth, offset
    for s in range(n):
        here = s == me
        prior_growth = jnp.where(here, growth, prior_growth)
        prior_offset = jnp.where(here, offset, prior_offset)
        own = maps[s]
        offset = own[:levels] * offset + own[levels:]
        growth = growth * own[:levels]
    wrap = offset / (1.0 - growth)
    entry[...] = prior_growth * wrap + prior_offset

    areas = jnp.broadcast_to(area[...], (levels, rows))
    row = lane_index((levels, rows))
    masked = polar & (row >= row0) & (row < row0 + POLAR)
    part[lat, :levels] = jnp.where(masked, 0.0, areas * wrap)
    part[lat, levels:] = areas

    def take_back():
        wait(back, b_sem.at[1], peers)
        total = jnp.zeros((levels, LANES), jnp.float32)
        sub = lax.broadcasted_iota(jnp.int32, (levels, LANES), 0)
        for l in range(levels):
            total = jnp.where(sub == l, back[l, POLAR : POLAR + 1, :LANES], total)
        first_lane = lane_index((levels, LANES)) == 0
        part[lat, :levels, :LANES] = part[lat, :levels, :LANES] + jnp.where(first_lane, total, 0.0)

    def send_part():
        @pl.loop(1, z)
        def _(k):
            send(part.at[lat], part.at[lat], d_sem, k, "lat")

    pl.when(jnp.logical_not(polar))(send_part)

    @pl.loop(0, levels, step=GROUP)
    def _(first):
        @pl.when(polar & (first == GROUP))
        def _():
            take_back()
            send_part()

        for l in range(GROUP):
            flow = bg[first + l] * entry[pl.ds(first + l, 1), :] + bo[first + l]
            for v in range(steps):
                ct[first + l, pl.ds(v, CHUNKS, stride=steps), :] = gs[v, first + l] * flow + os[v, first + l]
            for h in range(halves):
                c = pl.ds(h * LANES, LANES)
                updated[first + l, :, c] = jnp.transpose(ct[first + l, c, :]) * cov[first + l, :, c]

    @pl.when(polar)
    def _():
        for l in range(levels):
            updated[l, slab, :] = back[l, :POLAR, :]
        wait(slabs, p_sem.at[0], peers)
        is_worker(me, lambda: wait(pu, b_sem.at[0], n - 1))

    wait(maps, m_sem.at[0], n - 1)
    wait(part, d_sem.at[0], z - 1)
    wait(part, d_sem.at[1], z - 1)
    total = part[0]
    for s in range(1, z):
        total = total + part[s]
    sums = jnp.sum(total, axis=1, keepdims=True)
    mean = jnp.broadcast_to(sums[:levels] / sums[levels:], (levels, LANES))
    diagonal = lax.broadcasted_iota(jnp.int32, (levels, LANES), 0) == lane_index((levels, LANES))
    dateline[...] = jnp.sum(jnp.where(diagonal, mean, 0.0), axis=0, keepdims=True)[:, :levels]


def write_out(updated_in, dateline_in, updated, dateline, sem):
    copies = (
        pltpu.make_async_copy(updated_in, updated, sem.at[0]),
        pltpu.make_async_copy(dateline_in, dateline, sem.at[1]),
    )
    for copy in copies:
        copy.start()
    for copy in copies:
        copy.wait()


def body(n, z, tracer, courant, hop_counts, row_area):
    levels, rows, cells = tracer.shape
    f32 = jnp.float32
    vmem = pl.BlockSpec(memory_space=pltpu.VMEM)
    hbm = pl.BlockSpec(memory_space=pl.ANY)
    dma = pltpu.SemaphoreType.DMA
    inputs = (tracer, courant, hop_counts.reshape(1, rows), row_area.reshape(1, rows))
    updated, dateline = pl.pallas_call(
        functools.partial(kernel, n, z),
        out_shape=(
            pltpu.VMEM(tracer.shape, f32),
            pltpu.VMEM((1, levels), f32),
        ),
        in_specs=[hbm] * 4,
        out_specs=(vmem, vmem),
        scratch_shapes=[
            pltpu.VMEM(tracer.shape, f32),
            pltpu.VMEM(tracer.shape, f32),
            pltpu.VMEM((cells, cells), jnp.bfloat16),
            pltpu.VMEM((levels, cells, rows), f32),
            pltpu.VMEM((levels, cells, rows), f32),
            pltpu.VMEM((cells // CHUNKS, levels, CHUNKS, rows), f32),
            pltpu.VMEM((cells // CHUNKS, levels, CHUNKS, rows), f32),
            pltpu.VMEM((levels, CHUNKS, rows), f32),
            pltpu.VMEM((levels, CHUNKS, rows), f32),
            pltpu.VMEM((levels, rows), f32),
            pltpu.VMEM((n, 2 * levels, rows), f32),
            pltpu.VMEM((levels, 2, POLAR, cells), f32),
            pltpu.VMEM((n, 2, POLAR, cells), f32),
            pltpu.VMEM((n, 2 * POLAR, cells), f32),
            pltpu.VMEM((levels, 2 * POLAR, cells), f32),
            pltpu.VMEM((z, 2 * levels, rows), f32),
            pltpu.VMEM((1, rows), jnp.int32),
            pltpu.VMEM((1, rows), f32),
            dma((2,)), dma((2, levels)), dma((2,)),
            dma((2,)), dma((2,)), dma((2,)), dma((2,)),
        ],
        compiler_params=pltpu.CompilerParams(
            collective_id=0, has_side_effects=True, vmem_limit_bytes=24 * 1024 * 1024
        ),
        cost_estimate=pl.CostEstimate(
            flops=60 * tracer.size, bytes_accessed=12 * tracer.size, transcendentals=tracer.size
        ),
    )(*(pltpu.with_memory_space_constraint(a, pltpu.HBM) for a in inputs))
    held = (pltpu.with_memory_space_constraint(a, pltpu.VMEM) for a in (updated, dateline))
    updated, dateline = pl.pallas_call(
        write_out,
        out_shape=(pltpu.HBM(tracer.shape, f32), pltpu.HBM((1, levels), f32)),
        in_specs=[hbm, hbm],
        out_specs=(hbm, hbm),
        scratch_shapes=[dma((2,))],
    )(*held)
    return updated, dateline.reshape(levels)


def solution(mesh):
    return jax.shard_map(
        functools.partial(body, mesh.shape["lon"], mesh.shape["lat"]),
        mesh=mesh,
        in_specs=(P(None, "lat", "lon"), P(None, "lat", "lon"), P("lat"), P("lat")),
        out_specs=(P(None, "lat", "lon"), P()),
        check_vma=False,
    )
```

```python
import functools

import jax
import jax.numpy as jnp
from jax import lax
from jax.experimental import pallas as pl
from jax.experimental.pallas import tpu as pltpu
from jax.sharding import PartitionSpec as P

POLAR = 8
STOPS = 7
LANES = 128
CHUNKS = 8
GROUP = 2
EARLY = 2


def lane_index(shape):
    return lax.broadcasted_iota(jnp.int32, shape, len(shape) - 1)


def scan_lanes(growth, offset):
    lane = lane_index(growth.shape)
    stride = 1
    while stride < LANES:
        inside = lane >= stride
        lead_growth = pltpu.roll(growth, stride, 1)
        lead_offset = pltpu.roll(offset, stride, 1)
        offset = jnp.where(inside, growth * lead_offset + offset, offset)
        growth = jnp.where(inside, growth * lead_growth, growth)
        stride *= 2
    return growth, offset


def solve_block(courants, sources):
    out, end = [], None
    for courant, source in zip(courants, sources):
        above = 1.0 + courant
        shared = 1.0 / (courant * above)
        ratio = 1.0 - shared * courant
        inverse = shared * above
        growth, offset = scan_lanes(ratio, ratio * source)
        if end is not None:
            offset = growth * end[1] + offset
            growth = growth * end[0]
        end = (
            jnp.broadcast_to(growth[:, LANES - 1 :], growth.shape),
            jnp.broadcast_to(offset[:, LANES - 1 :], offset.shape),
        )
        out.append((growth * inverse, offset * inverse))
    return out, end


def kernel(
    n, z, tracer, courant, hops_in, area_in, updated, dateline,
    trv, cov, st, ct, gs, os, bg, bo, entry, maps, slabs, pin, pu, back, part, hops, area,
    small_sem, in_sem, slab_sem, p_sem, m_sem, b_sem, d_sem,
):
    levels, rows, cells = trv.shape
    halves = cells // LANES
    steps = cells // CHUNKS
    me = lax.axis_index("lon")
    lat = lax.axis_index("lat")
    polar = (lat == 0) | (lat == z - 1)
    row0 = pl.multiple_of(jnp.where(lat == 0, 0, rows - POLAR), POLAR)
    slab = pl.ds(row0, POLAR)
    own_level = lax.rem(me, levels)
    every = n == levels
    peers = n - 1 if every else levels - jnp.where(me < levels, 1, 0)

    def ahead(k):
        return lax.rem(me + k, n)

    def is_worker(device, work):
        if every:
            work()
        else:
            pl.when(device < levels)(work)

    barrier = pltpu.get_barrier_semaphore()

    @pl.loop(1, n)
    def _(k):
        pl.semaphore_signal(barrier, inc=1, device_id={"lon": ahead(k)}, device_id_type=pl.DeviceIdType.MESH)

    @pl.loop(1, z)
    def _(k):
        pl.semaphore_signal(
            barrier, inc=1, device_id={"lat": lax.rem(lat + k, z)}, device_id_type=pl.DeviceIdType.MESH
        )

    def load_slabs():
        return (
            pltpu.make_async_copy(courant.at[:, slab], slabs.at[:, 0], slab_sem.at[0]),
            pltpu.make_async_copy(tracer.at[:, slab], slabs.at[:, 1], slab_sem.at[1]),
        )

    @pl.when(polar)
    def _():
        for copy in load_slabs():
            copy.start()

    def load(l):
        some = pl.ds(l, GROUP)
        return (
            pltpu.make_async_copy(tracer.at[some], trv.at[some], in_sem.at[0, l]),
            pltpu.make_async_copy(courant.at[some], cov.at[some], in_sem.at[1, l]),
        )

    for l in range(0, levels, GROUP):
        for copy in load(l):
            copy.start()
    small = (
        pltpu.make_async_copy(hops_in, hops, small_sem.at[0]),
        pltpu.make_async_copy(area_in, area, small_sem.at[1]),
    )
    for copy in small:
        copy.start()

    def send(source, target, sem, k, axis="lon"):
        place = ahead(k) if axis == "lon" else lax.rem(lat + k, z)
        pltpu.make_async_remote_copy(
            src_ref=source, dst_ref=target, send_sem=sem.at[0], recv_sem=sem.at[1],
            device_id={axis: place}, device_id_type=pl.DeviceIdType.MESH,
        ).start()

    def wait(slots, sem, count):
        if isinstance(count, int):
            some = slots.at[pl.ds(0, count)]
            pltpu.make_async_copy(some, some, sem).wait()
        else:
            @pl.loop(0, count)
            def _(_):
                pltpu.make_async_copy(slots.at[0], slots.at[0], sem).wait()

    def turn(first):
        for copy in load(first):
            copy.wait()
        for l in range(GROUP):
            for h in range(halves):
                c = pl.ds(h * LANES, LANES)
                here = cov[first + l, :, c]
                above = 1.0 + here
                shared = 1.0 / (here * above)
                ratio = 1.0 - shared * here
                cov[first + l, :, c] = shared * above
                ct[first + l, c, :] = jnp.transpose(ratio)
                st[first + l, c, :] = jnp.transpose(ratio * trv[first + l, :, c])

    early = levels * EARLY // 8 // GROUP * GROUP
    pl.loop(0, early, step=GROUP)(turn)

    pl.semaphore_wait(barrier, n + z - 2)

    @pl.when(polar)
    def _():
        for copy in load_slabs():
            copy.wait()

        @pl.loop(1, n)
        def _(k):
            is_worker(ahead(k), lambda: send(slabs.at[lax.rem(ahead(k), levels)], pin.at[me], p_sem, k))

        pin[me] = slabs[own_level]

    pl.loop(early, levels, step=GROUP)(turn)

    def step(v, state):
        growth, offset = state
        cells_v = pl.ds(v, CHUNKS, stride=steps)
        ratio = ct[:, cells_v, :]
        growth = growth * ratio
        offset = ratio * offset + st[:, cells_v, :]
        gs[v] = growth
        os[v] = offset
        return growth, offset

    shape = (levels, CHUNKS, rows)
    growth, offset = lax.fori_loop(
        0, steps, step, (jnp.ones(shape, jnp.float32), jnp.zeros(shape, jnp.float32)), unroll=4
    )
    for copy in small:
        copy.wait()
    sub = lax.broadcasted_iota(jnp.int32, (CHUNKS, rows), 0)
    whole = []
    for l in range(levels):
        g, o = growth[l], offset[l]
        stride = 1
        while stride < CHUNKS:
            inside = sub >= stride
            lead_g, lead_o = pltpu.roll(g, stride, 0), pltpu.roll(o, stride, 0)
            o = jnp.where(inside, g * lead_o + o, o)
            g = jnp.where(inside, g * lead_g, g)
            stride *= 2
        maps[me, l : l + 1, :] = g[CHUNKS - 1 :]
        maps[me, levels + l : levels + l + 1, :] = o[CHUNKS - 1 :]
        whole.append((g, o))

    @pl.loop(1, n)
    def _(k):
        send(maps.at[me], maps.at[me], m_sem, k)

    for l, (g, o) in enumerate(whole):
        bg[l] = jnp.where(sub == 0, 1.0, pltpu.roll(g, 1, 0))
        bo[l] = jnp.where(sub == 0, 0.0, pltpu.roll(o, 1, 0))

    def column(values):
        place = lane_index((POLAR, rows)) == lax.broadcasted_iota(jnp.int32, (POLAR, rows), 0) + row0
        return jnp.sum(jnp.where(place, jnp.broadcast_to(values, (POLAR, rows)), 0.0), axis=1, keepdims=True)

    def solve_polar():
        count = jnp.broadcast_to(column(hops[...].astype(jnp.float32)), (POLAR, LANES)).astype(jnp.int32)
        weights = column(area[...])
        wait(pin, p_sem.at[1], n - 1)
        courants, sources = [], []
        for h in range(halves):
            c = pl.ds(h * LANES, LANES)
            blocks = [pin[s, 1, :, c] for s in range(n)]
            for bit in range(STOPS.bit_length()):
                chosen = jnp.right_shift(count, bit) % 2 == 1
                blocks = [
                    jnp.where(chosen, blocks[(s - (1 << bit)) % n], blocks[s]) for s in range(n)
                ]
            sources.append(jnp.concatenate(blocks, axis=0))
            courants.append(jnp.concatenate([pin[s, 0, :, c] for s in range(n)], axis=0))
        out, end = solve_block(courants, sources)
        growth = jnp.ones((POLAR, LANES), jnp.float32)
        offset = jnp.zeros((POLAR, LANES), jnp.float32)
        prior = []
        for s in range(n):
            prior.append((growth, offset))
            own = slice(s * POLAR, (s + 1) * POLAR)
            offset = end[0][own] * offset + end[1][own]
            growth = growth * end[0][own]
        wrap = offset / (1.0 - growth)
        weighted = jnp.broadcast_to(jnp.sum(weights * wrap, axis=0, keepdims=True), (POLAR, LANES))
        for s in range(n):
            inflow = prior[s][0] * wrap + prior[s][1]
            own = slice(s * POLAR, (s + 1) * POLAR)
            for h, (g, o) in enumerate(out):
                c = pl.ds(h * LANES, LANES)
                pu[s, :POLAR, c] = g[own] * inflow + o[own]
                pu[s, POLAR:, c] = weighted

        @pl.loop(1, n)
        def _(k):
            send(pu.at[ahead(k)], back.at[own_level], b_sem, k)

        back[own_level] = pu[me]

    @pl.when(polar)
    def _():
        is_worker(me, solve_polar)

    wait(maps, m_sem.at[1], n - 1)
    growth = jnp.ones((levels, rows), jnp.float32)
    offset = jnp.zeros((levels, rows), jnp.float32)
    prior_growth, prior_offset = growth, offset
    for s in range(n):
        here = s == me
        prior_growth = jnp.where(here, growth, prior_growth)
        prior_offset = jnp.where(here, offset, prior_offset)
        own = maps[s]
        offset = own[:levels] * offset + own[levels:]
        growth = growth * own[:levels]
    wrap = offset / (1.0 - growth)
    entry[...] = prior_growth * wrap + prior_offset

    areas = jnp.broadcast_to(area[...], (levels, rows))
    row = lane_index((levels, rows))
    masked = polar & (row >= row0) & (row < row0 + POLAR)
    part[lat, :levels] = jnp.where(masked, 0.0, areas * wrap)
    part[lat, levels:] = areas

    def take_back():
        wait(back, b_sem.at[1], peers)
        total = jnp.zeros((levels, LANES), jnp.float32)
        sub = lax.broadcasted_iota(jnp.int32, (levels, LANES), 0)
        for l in range(levels):
            total = jnp.where(sub == l, back[l, POLAR : POLAR + 1, :LANES], total)
        first_lane = lane_index((levels, LANES)) == 0
        part[lat, :levels, :LANES] = part[lat, :levels, :LANES] + jnp.where(first_lane, total, 0.0)

    def send_part():
        @pl.loop(1, z)
        def _(k):
            send(part.at[lat], part.at[lat], d_sem, k, "lat")

    pl.when(jnp.logical_not(polar))(send_part)

    @pl.loop(0, levels, step=GROUP)
    def _(first):
        @pl.when(polar & (first == GROUP))
        def _():
            take_back()
            send_part()

        for l in range(GROUP):
            flow = bg[first + l] * entry[pl.ds(first + l, 1), :] + bo[first + l]
            for v in range(steps):
                ct[first + l, pl.ds(v, CHUNKS, stride=steps), :] = gs[v, first + l] * flow + os[v, first + l]
            for h in range(halves):
                c = pl.ds(h * LANES, LANES)
                updated[first + l, :, c] = jnp.transpose(ct[first + l, c, :]) * cov[first + l, :, c]

    @pl.when(polar)
    def _():
        for l in range(levels):
            updated[l, slab, :] = back[l, :POLAR, :]
        wait(slabs, p_sem.at[0], peers)
        is_worker(me, lambda: wait(pu, b_sem.at[0], n - 1))

    wait(maps, m_sem.at[0], n - 1)
    wait(part, d_sem.at[0], z - 1)
    wait(part, d_sem.at[1], z - 1)
    total = part[0]
    for s in range(1, z):
        total = total + part[s]
    sums = jnp.sum(total, axis=1, keepdims=True)
    mean = jnp.broadcast_to(sums[:levels] / sums[levels:], (levels, LANES))
    diagonal = lax.broadcasted_iota(jnp.int32, (levels, LANES), 0) == lane_index((levels, LANES))
    dateline[...] = jnp.sum(jnp.where(diagonal, mean, 0.0), axis=0, keepdims=True)[:, :levels]


def write_out(updated_in, dateline_in, updated, dateline, sem):
    copies = (
        pltpu.make_async_copy(updated_in, updated, sem.at[0]),
        pltpu.make_async_copy(dateline_in, dateline, sem.at[1]),
    )
    for copy in copies:
        copy.start()
    for copy in copies:
        copy.wait()


def body(n, z, tracer, courant, hop_counts, row_area):
    levels, rows, cells = tracer.shape
    f32 = jnp.float32
    vmem = pl.BlockSpec(memory_space=pltpu.VMEM)
    hbm = pl.BlockSpec(memory_space=pl.ANY)
    dma = pltpu.SemaphoreType.DMA
    inputs = (tracer, courant, hop_counts.reshape(1, rows), row_area.reshape(1, rows))
    updated, dateline = pl.pallas_call(
        functools.partial(kernel, n, z),
        out_shape=(
            pltpu.VMEM(tracer.shape, f32),
            pltpu.VMEM((1, levels), f32),
        ),
        in_specs=[hbm] * 4,
        out_specs=(vmem, vmem),
        scratch_shapes=[
            pltpu.VMEM(tracer.shape, f32),
            pltpu.VMEM(tracer.shape, f32),
            pltpu.VMEM((levels, cells, rows), f32),
            pltpu.VMEM((levels, cells, rows), f32),
            pltpu.VMEM((cells // CHUNKS, levels, CHUNKS, rows), f32),
            pltpu.VMEM((cells // CHUNKS, levels, CHUNKS, rows), f32),
            pltpu.VMEM((levels, CHUNKS, rows), f32),
            pltpu.VMEM((levels, CHUNKS, rows), f32),
            pltpu.VMEM((levels, rows), f32),
            pltpu.VMEM((n, 2 * levels, rows), f32),
            pltpu.VMEM((levels, 2, POLAR, cells), f32),
            pltpu.VMEM((n, 2, POLAR, cells), f32),
            pltpu.VMEM((n, 2 * POLAR, cells), f32),
            pltpu.VMEM((levels, 2 * POLAR, cells), f32),
            pltpu.VMEM((z, 2 * levels, rows), f32),
            pltpu.VMEM((1, rows), jnp.int32),
            pltpu.VMEM((1, rows), f32),
            dma((2,)), dma((2, levels)), dma((2,)),
            dma((2,)), dma((2,)), dma((2,)), dma((2,)),
        ],
        compiler_params=pltpu.CompilerParams(
            collective_id=0, has_side_effects=True, vmem_limit_bytes=24 * 1024 * 1024
        ),
        cost_estimate=pl.CostEstimate(
            flops=60 * tracer.size, bytes_accessed=12 * tracer.size, transcendentals=tracer.size
        ),
    )(*(pltpu.with_memory_space_constraint(a, pltpu.HBM) for a in inputs))
    held = (pltpu.with_memory_space_constraint(a, pltpu.VMEM) for a in (updated, dateline))
    updated, dateline = pl.pallas_call(
        write_out,
        out_shape=(pltpu.HBM(tracer.shape, f32), pltpu.HBM((1, levels), f32)),
        in_specs=[hbm, hbm],
        out_specs=(hbm, hbm),
        scratch_shapes=[dma((2,))],
    )(*held)
    return updated, dateline.reshape(levels)


def solution(mesh):
    return jax.shard_map(
        functools.partial(body, mesh.shape["lon"], mesh.shape["lat"]),
        mesh=mesh,
        in_specs=(P(None, "lat", "lon"), P(None, "lat", "lon"), P("lat"), P("lat")),
        out_specs=(P(None, "lat", "lon"), P()),
        check_vma=False,
    )
```

```python
import functools

import jax
import jax.numpy as jnp
from jax import lax
from jax.experimental import pallas as pl
from jax.experimental.pallas import tpu as pltpu
from jax.sharding import PartitionSpec as P

POLAR = 8
STOPS = 7
LANES = 128
CHUNKS = 8
GROUP = 2
EARLY = 2


def lane_index(shape):
    return lax.broadcasted_iota(jnp.int32, shape, len(shape) - 1)


def scan_lanes(growth, offset):
    lane = lane_index(growth.shape)
    stride = 1
    while stride < LANES:
        inside = lane >= stride
        lead_growth = pltpu.roll(growth, stride, 1)
        lead_offset = pltpu.roll(offset, stride, 1)
        offset = jnp.where(inside, growth * lead_offset + offset, offset)
        growth = jnp.where(inside, growth * lead_growth, growth)
        stride *= 2
    return growth, offset


def solve_block(courants, sources):
    out, end = [], None
    for courant, source in zip(courants, sources):
        above = 1.0 + courant
        shared = 1.0 / (courant * above)
        ratio = 1.0 - shared * courant
        inverse = shared * above
        growth, offset = scan_lanes(ratio, ratio * source)
        if end is not None:
            offset = growth * end[1] + offset
            growth = growth * end[0]
        end = (
            jnp.broadcast_to(growth[:, LANES - 1 :], growth.shape),
            jnp.broadcast_to(offset[:, LANES - 1 :], offset.shape),
        )
        out.append((growth * inverse, offset * inverse))
    return out, end


def kernel(
    n, z, tracer, courant, hops_in, area_in, updated, dateline,
    trv, cov, st, ct, gs, os, bg, bo, entry, maps, slabs, pin, pu, back, part, hops, area,
    small_sem, in_sem, slab_sem, p_sem, m_sem, b_sem, d_sem,
):
    levels, rows, cells = trv.shape
    halves = cells // LANES
    steps = cells // CHUNKS
    me = lax.axis_index("lon")
    lat = lax.axis_index("lat")
    polar = (lat == 0) | (lat == z - 1)
    row0 = pl.multiple_of(jnp.where(lat == 0, 0, rows - POLAR), POLAR)
    slab = pl.ds(row0, POLAR)
    own_level = lax.rem(me, levels)
    every = n == levels
    peers = n - 1 if every else levels - jnp.where(me < levels, 1, 0)

    def ahead(k):
        return lax.rem(me + k, n)

    def is_worker(device, work):
        if every:
            work()
        else:
            pl.when(device < levels)(work)

    barrier = pltpu.get_barrier_semaphore()

    @pl.loop(1, n)
    def _(k):
        pl.semaphore_signal(barrier, inc=1, device_id={"lon": ahead(k)}, device_id_type=pl.DeviceIdType.MESH)

    @pl.loop(1, z)
    def _(k):
        pl.semaphore_signal(
            barrier, inc=1, device_id={"lat": lax.rem(lat + k, z)}, device_id_type=pl.DeviceIdType.MESH
        )

    def load_slabs():
        return (
            pltpu.make_async_copy(courant.at[:, slab], slabs.at[:, 0], slab_sem.at[0]),
            pltpu.make_async_copy(tracer.at[:, slab], slabs.at[:, 1], slab_sem.at[1]),
        )

    @pl.when(polar)
    def _():
        for copy in load_slabs():
            copy.start()

    def load(l):
        some = pl.ds(l, GROUP)
        return (
            pltpu.make_async_copy(tracer.at[some], trv.at[some], in_sem.at[0, l]),
            pltpu.make_async_copy(courant.at[some], cov.at[some], in_sem.at[1, l]),
        )

    for l in range(0, levels, GROUP):
        for copy in load(l):
            copy.start()
    small = (
        pltpu.make_async_copy(hops_in, hops, small_sem.at[0]),
        pltpu.make_async_copy(area_in, area, small_sem.at[1]),
    )
    for copy in small:
        copy.start()

    def send(source, target, sem, k, axis="lon"):
        place = ahead(k) if axis == "lon" else lax.rem(lat + k, z)
        pltpu.make_async_remote_copy(
            src_ref=source, dst_ref=target, send_sem=sem.at[0], recv_sem=sem.at[1],
            device_id={axis: place}, device_id_type=pl.DeviceIdType.MESH,
        ).start()

    def wait(slots, sem, count):
        if isinstance(count, int):
            some = slots.at[pl.ds(0, count)]
            pltpu.make_async_copy(some, some, sem).wait()
        else:
            @pl.loop(0, count)
            def _(_):
                pltpu.make_async_copy(slots.at[0], slots.at[0], sem).wait()

    def turn(first):
        for copy in load(first):
            copy.wait()
        for l in range(GROUP):
            for h in range(halves):
                c = pl.ds(h * LANES, LANES)
                here = cov[first + l, :, c]
                above = 1.0 + here
                shared = 1.0 / (here * above)
                ratio = 1.0 - shared * here
                cov[first + l, :, c] = shared * above
                ct[first + l, c, :] = jnp.transpose(ratio)
                st[first + l, c, :] = jnp.transpose(ratio * trv[first + l, :, c])

    early = levels * EARLY // 8 // GROUP * GROUP
    pl.loop(0, early, step=GROUP)(turn)

    pl.semaphore_wait(barrier, n + z - 2)

    @pl.when(polar)
    def _():
        for copy in load_slabs():
            copy.wait()

        @pl.loop(1, n)
        def _(k):
            is_worker(ahead(k), lambda: send(slabs.at[lax.rem(ahead(k), levels)], pin.at[me], p_sem, k))

        pin[me] = slabs[own_level]

    pl.loop(early, levels, step=GROUP)(turn)

    def step(v, state):
        growth, offset = state
        cells_v = pl.ds(v, CHUNKS, stride=steps)
        ratio = ct[:, cells_v, :]
        growth = growth * ratio
        offset = ratio * offset + st[:, cells_v, :]
        gs[v] = growth
        os[v] = offset
        return growth, offset

    shape = (levels, CHUNKS, rows)
    growth, offset = lax.fori_loop(
        0, steps, step, (jnp.ones(shape, jnp.float32), jnp.zeros(shape, jnp.float32)), unroll=4
    )
    for copy in small:
        copy.wait()
    sub = lax.broadcasted_iota(jnp.int32, (CHUNKS, rows), 0)
    whole = []
    for l in range(levels):
        g, o = growth[l], offset[l]
        stride = 1
        while stride < CHUNKS:
            inside = sub >= stride
            lead_g, lead_o = pltpu.roll(g, stride, 0), pltpu.roll(o, stride, 0)
            o = jnp.where(inside, g * lead_o + o, o)
            g = jnp.where(inside, g * lead_g, g)
            stride *= 2
        maps[me, l : l + 1, :] = g[CHUNKS - 1 :]
        maps[me, levels + l : levels + l + 1, :] = o[CHUNKS - 1 :]
        whole.append((g, o))

    @pl.loop(1, n)
    def _(k):
        send(maps.at[me], maps.at[me], m_sem, k)

    for l, (g, o) in enumerate(whole):
        bg[l] = jnp.where(sub == 0, 1.0, pltpu.roll(g, 1, 0))
        bo[l] = jnp.where(sub == 0, 0.0, pltpu.roll(o, 1, 0))

    def column(values):
        place = lane_index((POLAR, rows)) == lax.broadcasted_iota(jnp.int32, (POLAR, rows), 0) + row0
        return jnp.sum(jnp.where(place, jnp.broadcast_to(values, (POLAR, rows)), 0.0), axis=1, keepdims=True)

    def solve_polar():
        count = jnp.broadcast_to(column(hops[...].astype(jnp.float32)), (POLAR, LANES)).astype(jnp.int32)
        weights = column(area[...])
        wait(pin, p_sem.at[1], n - 1)
        courants, sources = [], []
        for h in range(halves):
            c = pl.ds(h * LANES, LANES)
            blocks = [pin[s, 1, :, c] for s in range(n)]
            for bit in range(STOPS.bit_length()):
                chosen = jnp.right_shift(count, bit) % 2 == 1
                blocks = [
                    jnp.where(chosen, blocks[(s - (1 << bit)) % n], blocks[s]) for s in range(n)
                ]
            sources.append(jnp.concatenate(blocks, axis=0))
            courants.append(jnp.concatenate([pin[s, 0, :, c] for s in range(n)], axis=0))
        out, end = solve_block(courants, sources)
        growth = jnp.ones((POLAR, LANES), jnp.float32)
        offset = jnp.zeros((POLAR, LANES), jnp.float32)
        prior = []
        for s in range(n):
            prior.append((growth, offset))
            own = slice(s * POLAR, (s + 1) * POLAR)
            offset = end[0][own] * offset + end[1][own]
            growth = growth * end[0][own]
        wrap = offset / (1.0 - growth)
        weighted = jnp.broadcast_to(jnp.sum(weights * wrap, axis=0, keepdims=True), (POLAR, LANES))
        for s in range(n):
            inflow = prior[s][0] * wrap + prior[s][1]
            own = slice(s * POLAR, (s + 1) * POLAR)
            for h, (g, o) in enumerate(out):
                pu[s, h * POLAR : (h + 1) * POLAR, :] = g[own] * inflow + o[own]
            pu[s, halves * POLAR :, :] = weighted

        @pl.loop(1, n)
        def _(k):
            send(pu.at[ahead(k)], back.at[own_level], b_sem, k)

        back[own_level] = pu[me]

    @pl.when(polar)
    def _():
        is_worker(me, solve_polar)

    wait(maps, m_sem.at[1], n - 1)
    growth = jnp.ones((levels, rows), jnp.float32)
    offset = jnp.zeros((levels, rows), jnp.float32)
    prior_growth, prior_offset = growth, offset
    for s in range(n):
        here = s == me
        prior_growth = jnp.where(here, growth, prior_growth)
        prior_offset = jnp.where(here, offset, prior_offset)
        own = maps[s]
        offset = own[:levels] * offset + own[levels:]
        growth = growth * own[:levels]
    wrap = offset / (1.0 - growth)
    entry[...] = prior_growth * wrap + prior_offset

    areas = jnp.broadcast_to(area[...], (levels, rows))
    row = lane_index((levels, rows))
    masked = polar & (row >= row0) & (row < row0 + POLAR)
    part[lat, :levels] = jnp.where(masked, 0.0, areas * wrap)
    part[lat, levels:] = areas

    def take_back():
        wait(back, b_sem.at[1], peers)
        total = jnp.zeros((levels, LANES), jnp.float32)
        sub = lax.broadcasted_iota(jnp.int32, (levels, LANES), 0)
        for l in range(levels):
            total = jnp.where(sub == l, back[l, halves * POLAR : halves * POLAR + 1, :], total)
        first_lane = lane_index((levels, LANES)) == 0
        part[lat, :levels, :LANES] = part[lat, :levels, :LANES] + jnp.where(first_lane, total, 0.0)

    def send_part():
        @pl.loop(1, z)
        def _(k):
            send(part.at[lat], part.at[lat], d_sem, k, "lat")

    pl.when(jnp.logical_not(polar))(send_part)

    @pl.loop(0, levels, step=GROUP)
    def _(first):
        @pl.when(polar & (first == GROUP))
        def _():
            take_back()
            send_part()

        for l in range(GROUP):
            flow = bg[first + l] * entry[pl.ds(first + l, 1), :] + bo[first + l]
            for v in range(steps):
                ct[first + l, pl.ds(v, CHUNKS, stride=steps), :] = gs[v, first + l] * flow + os[v, first + l]
            for h in range(halves):
                c = pl.ds(h * LANES, LANES)
                updated[first + l, :, c] = jnp.transpose(ct[first + l, c, :]) * cov[first + l, :, c]

    @pl.when(polar)
    def _():
        for l in range(levels):
            for h in range(halves):
                updated[l, slab, pl.ds(h * LANES, LANES)] = back[l, h * POLAR : (h + 1) * POLAR, :]
        wait(slabs, p_sem.at[0], peers)
        is_worker(me, lambda: wait(pu, b_sem.at[0], n - 1))

    wait(maps, m_sem.at[0], n - 1)
    wait(part, d_sem.at[0], z - 1)
    wait(part, d_sem.at[1], z - 1)
    total = part[0]
    for s in range(1, z):
        total = total + part[s]
    sums = jnp.sum(total, axis=1, keepdims=True)
    mean = jnp.broadcast_to(sums[:levels] / sums[levels:], (levels, LANES))
    diagonal = lax.broadcasted_iota(jnp.int32, (levels, LANES), 0) == lane_index((levels, LANES))
    dateline[...] = jnp.sum(jnp.where(diagonal, mean, 0.0), axis=0, keepdims=True)[:, :levels]


def write_out(updated_in, dateline_in, updated, dateline, sem):
    copies = (
        pltpu.make_async_copy(updated_in, updated, sem.at[0]),
        pltpu.make_async_copy(dateline_in, dateline, sem.at[1]),
    )
    for copy in copies:
        copy.start()
    for copy in copies:
        copy.wait()


def body(n, z, tracer, courant, hop_counts, row_area):
    levels, rows, cells = tracer.shape
    f32 = jnp.float32
    vmem = pl.BlockSpec(memory_space=pltpu.VMEM)
    hbm = pl.BlockSpec(memory_space=pl.ANY)
    dma = pltpu.SemaphoreType.DMA
    inputs = (tracer, courant, hop_counts.reshape(1, rows), row_area.reshape(1, rows))
    updated, dateline = pl.pallas_call(
        functools.partial(kernel, n, z),
        out_shape=(
            pltpu.VMEM(tracer.shape, f32),
            pltpu.VMEM((1, levels), f32),
        ),
        in_specs=[hbm] * 4,
        out_specs=(vmem, vmem),
        scratch_shapes=[
            pltpu.VMEM(tracer.shape, f32),
            pltpu.VMEM(tracer.shape, f32),
            pltpu.VMEM((levels, cells, rows), f32),
            pltpu.VMEM((levels, cells, rows), f32),
            pltpu.VMEM((cells // CHUNKS, levels, CHUNKS, rows), f32),
            pltpu.VMEM((cells // CHUNKS, levels, CHUNKS, rows), f32),
            pltpu.VMEM((levels, CHUNKS, rows), f32),
            pltpu.VMEM((levels, CHUNKS, rows), f32),
            pltpu.VMEM((levels, rows), f32),
            pltpu.VMEM((n, 2 * levels, rows), f32),
            pltpu.VMEM((levels, 2, POLAR, cells), f32),
            pltpu.VMEM((n, 2, POLAR, cells), f32),
            pltpu.VMEM((n, (cells // LANES + 1) * POLAR, LANES), f32),
            pltpu.VMEM((levels, (cells // LANES + 1) * POLAR, LANES), f32),
            pltpu.VMEM((z, 2 * levels, rows), f32),
            pltpu.VMEM((1, rows), jnp.int32),
            pltpu.VMEM((1, rows), f32),
            dma((2,)), dma((2, levels)), dma((2,)),
            dma((2,)), dma((2,)), dma((2,)), dma((2,)),
        ],
        compiler_params=pltpu.CompilerParams(
            collective_id=0, has_side_effects=True, vmem_limit_bytes=24 * 1024 * 1024
        ),
        cost_estimate=pl.CostEstimate(
            flops=60 * tracer.size, bytes_accessed=12 * tracer.size, transcendentals=tracer.size
        ),
    )(*(pltpu.with_memory_space_constraint(a, pltpu.HBM) for a in inputs))
    held = (pltpu.with_memory_space_constraint(a, pltpu.VMEM) for a in (updated, dateline))
    updated, dateline = pl.pallas_call(
        write_out,
        out_shape=(pltpu.HBM(tracer.shape, f32), pltpu.HBM((1, levels), f32)),
        in_specs=[hbm, hbm],
        out_specs=(hbm, hbm),
        scratch_shapes=[dma((2,))],
    )(*held)
    return updated, dateline.reshape(levels)


def solution(mesh):
    return jax.shard_map(
        functools.partial(body, mesh.shape["lon"], mesh.shape["lat"]),
        mesh=mesh,
        in_specs=(P(None, "lat", "lon"), P(None, "lat", "lon"), P("lat"), P("lat")),
        out_specs=(P(None, "lat", "lon"), P()),
        check_vma=False,
    )
```

```python
import functools

import jax
import jax.numpy as jnp
from jax import lax
from jax.experimental import pallas as pl
from jax.experimental.pallas import tpu as pltpu
from jax.sharding import PartitionSpec as P

POLAR = 8
STOPS = 7
LANES = 128
CHUNKS = 8
GROUP = 2
EARLY = 2


def lane_index(shape):
    return lax.broadcasted_iota(jnp.int32, shape, len(shape) - 1)


def scan_lanes(growth, offset):
    lane = lane_index(growth.shape)
    stride = 1
    while stride < LANES:
        inside = lane >= stride
        lead_growth = pltpu.roll(growth, stride, 1)
        lead_offset = pltpu.roll(offset, stride, 1)
        offset = jnp.where(inside, growth * lead_offset + offset, offset)
        growth = jnp.where(inside, growth * lead_growth, growth)
        stride *= 2
    return growth, offset


def solve_block(courants, sources):
    out, end = [], None
    for courant, source in zip(courants, sources):
        above = 1.0 + courant
        shared = 1.0 / (courant * above)
        ratio = 1.0 - shared * courant
        inverse = shared * above
        growth, offset = scan_lanes(ratio, ratio * source)
        if end is not None:
            offset = growth * end[1] + offset
            growth = growth * end[0]
        end = (
            jnp.broadcast_to(growth[:, LANES - 1 :], growth.shape),
            jnp.broadcast_to(offset[:, LANES - 1 :], offset.shape),
        )
        out.append((growth * inverse, offset * inverse))
    return out, end


def kernel(
    n, z, tracer, courant, hops_in, area_in, updated, dateline,
    trv, cov, st, ct, gs, os, bg, bo, entry, maps, slabs, pin, pu, back, part, hops, area,
    small_sem, in_sem, slab_sem, p_sem, m_sem, b_sem, d_sem,
):
    levels, rows, cells = trv.shape
    halves = cells // LANES
    steps = cells // CHUNKS
    me = lax.axis_index("lon")
    lat = lax.axis_index("lat")
    polar = (lat == 0) | (lat == z - 1)
    row0 = pl.multiple_of(jnp.where(lat == 0, 0, rows - POLAR), POLAR)
    slab = pl.ds(row0, POLAR)
    own_level = lax.rem(me, levels)
    every = n == levels
    peers = n - 1 if every else levels - jnp.where(me < levels, 1, 0)

    def ahead(k):
        return lax.rem(me + k, n)

    def is_worker(device, work):
        if every:
            work()
        else:
            pl.when(device < levels)(work)

    barrier = pltpu.get_barrier_semaphore()

    @pl.loop(1, n)
    def _(k):
        pl.semaphore_signal(barrier, inc=1, device_id={"lon": ahead(k)}, device_id_type=pl.DeviceIdType.MESH)

    @pl.loop(1, z)
    def _(k):
        pl.semaphore_signal(
            barrier, inc=1, device_id={"lat": lax.rem(lat + k, z)}, device_id_type=pl.DeviceIdType.MESH
        )

    def load_slabs():
        return (
            pltpu.make_async_copy(courant.at[:, slab], slabs.at[:, 0], slab_sem.at[0]),
            pltpu.make_async_copy(tracer.at[:, slab], slabs.at[:, 1], slab_sem.at[1]),
        )

    @pl.when(polar)
    def _():
        for copy in load_slabs():
            copy.start()

    def load(l):
        some = pl.ds(l, GROUP)
        return (
            pltpu.make_async_copy(tracer.at[some], trv.at[some], in_sem.at[0, l]),
            pltpu.make_async_copy(courant.at[some], cov.at[some], in_sem.at[1, l]),
        )

    for l in range(0, levels, GROUP):
        for copy in load(l):
            copy.start()
    small = (
        pltpu.make_async_copy(hops_in, hops, small_sem.at[0]),
        pltpu.make_async_copy(area_in, area, small_sem.at[1]),
    )
    for copy in small:
        copy.start()

    def send(source, target, sem, k, axis="lon"):
        place = ahead(k) if axis == "lon" else lax.rem(lat + k, z)
        pltpu.make_async_remote_copy(
            src_ref=source, dst_ref=target, send_sem=sem.at[0], recv_sem=sem.at[1],
            device_id={axis: place}, device_id_type=pl.DeviceIdType.MESH,
        ).start()

    def wait(slots, sem, count):
        if isinstance(count, int):
            some = slots.at[pl.ds(0, count)]
            pltpu.make_async_copy(some, some, sem).wait()
        else:
            @pl.loop(0, count)
            def _(_):
                pltpu.make_async_copy(slots.at[0], slots.at[0], sem).wait()

    def turn(first):
        for copy in load(first):
            copy.wait()
        for l in range(GROUP):
            for h in range(halves):
                c = pl.ds(h * LANES, LANES)
                here = cov[first + l, :, c]
                above = 1.0 + here
                shared = 1.0 / (here * above)
                ratio = 1.0 - shared * here
                cov[first + l, :, c] = shared * above
                ct[first + l, c, :] = jnp.transpose(ratio)
                st[first + l, c, :] = jnp.transpose(ratio * trv[first + l, :, c])

    early = levels * EARLY // 8 // GROUP * GROUP
    pl.loop(0, early, step=GROUP)(turn)

    pl.semaphore_wait(barrier, n + z - 2)

    @pl.when(polar)
    def _():
        for copy in load_slabs():
            copy.wait()

        @pl.loop(1, n)
        def _(k):
            is_worker(ahead(k), lambda: send(slabs.at[lax.rem(ahead(k), levels)], pin.at[me], p_sem, k))

        pin[me] = slabs[own_level]

    pl.loop(early, levels, step=GROUP)(turn)

    for copy in small:
        copy.wait()

    def column(values):
        place = lane_index((POLAR, rows)) == lax.broadcasted_iota(jnp.int32, (POLAR, rows), 0) + row0
        return jnp.sum(jnp.where(place, jnp.broadcast_to(values, (POLAR, rows)), 0.0), axis=1, keepdims=True)

    def solve_polar():
        count = jnp.broadcast_to(column(hops[...].astype(jnp.float32)), (POLAR, LANES)).astype(jnp.int32)
        weights = column(area[...])
        wait(pin, p_sem.at[1], n - 1)
        courants, sources = [], []
        for h in range(halves):
            c = pl.ds(h * LANES, LANES)
            blocks = [pin[s, 1, :, c] for s in range(n)]
            for bit in range(STOPS.bit_length()):
                chosen = jnp.right_shift(count, bit) % 2 == 1
                blocks = [
                    jnp.where(chosen, blocks[(s - (1 << bit)) % n], blocks[s]) for s in range(n)
                ]
            sources.append(jnp.concatenate(blocks, axis=0))
            courants.append(jnp.concatenate([pin[s, 0, :, c] for s in range(n)], axis=0))
        out, end = solve_block(courants, sources)
        growth = jnp.ones((POLAR, LANES), jnp.float32)
        offset = jnp.zeros((POLAR, LANES), jnp.float32)
        prior = []
        for s in range(n):
            prior.append((growth, offset))
            own = slice(s * POLAR, (s + 1) * POLAR)
            offset = end[0][own] * offset + end[1][own]
            growth = growth * end[0][own]
        wrap = offset / (1.0 - growth)
        weighted = jnp.broadcast_to(jnp.sum(weights * wrap, axis=0, keepdims=True), (POLAR, LANES))
        for s in range(n):
            inflow = prior[s][0] * wrap + prior[s][1]
            own = slice(s * POLAR, (s + 1) * POLAR)
            for h, (g, o) in enumerate(out):
                pu[s, h * POLAR : (h + 1) * POLAR, :] = g[own] * inflow + o[own]
            pu[s, halves * POLAR :, :] = weighted

        @pl.loop(1, n)
        def _(k):
            send(pu.at[ahead(k)], back.at[own_level], b_sem, k)

        back[own_level] = pu[me]

    @pl.when(polar)
    def _():
        is_worker(me, solve_polar)

    def step(v, state):
        growth, offset = state
        cells_v = pl.ds(v, CHUNKS, stride=steps)
        ratio = ct[:, cells_v, :]
        growth = growth * ratio
        offset = ratio * offset + st[:, cells_v, :]
        gs[v] = growth
        os[v] = offset
        return growth, offset

    shape = (levels, CHUNKS, rows)
    growth, offset = lax.fori_loop(
        0, steps, step, (jnp.ones(shape, jnp.float32), jnp.zeros(shape, jnp.float32)), unroll=4
    )
    sub = lax.broadcasted_iota(jnp.int32, (CHUNKS, rows), 0)
    whole = []
    for l in range(levels):
        g, o = growth[l], offset[l]
        stride = 1
        while stride < CHUNKS:
            inside = sub >= stride
            lead_g, lead_o = pltpu.roll(g, stride, 0), pltpu.roll(o, stride, 0)
            o = jnp.where(inside, g * lead_o + o, o)
            g = jnp.where(inside, g * lead_g, g)
            stride *= 2
        maps[me, l : l + 1, :] = g[CHUNKS - 1 :]
        maps[me, levels + l : levels + l + 1, :] = o[CHUNKS - 1 :]
        whole.append((g, o))

    @pl.loop(1, n)
    def _(k):
        send(maps.at[me], maps.at[me], m_sem, k)

    for l, (g, o) in enumerate(whole):
        bg[l] = jnp.where(sub == 0, 1.0, pltpu.roll(g, 1, 0))
        bo[l] = jnp.where(sub == 0, 0.0, pltpu.roll(o, 1, 0))

    wait(maps, m_sem.at[1], n - 1)
    growth = jnp.ones((levels, rows), jnp.float32)
    offset = jnp.zeros((levels, rows), jnp.float32)
    prior_growth, prior_offset = growth, offset
    for s in range(n):
        here = s == me
        prior_growth = jnp.where(here, growth, prior_growth)
        prior_offset = jnp.where(here, offset, prior_offset)
        own = maps[s]
        offset = own[:levels] * offset + own[levels:]
        growth = growth * own[:levels]
    wrap = offset / (1.0 - growth)
    entry[...] = prior_growth * wrap + prior_offset

    areas = jnp.broadcast_to(area[...], (levels, rows))
    row = lane_index((levels, rows))
    masked = polar & (row >= row0) & (row < row0 + POLAR)
    part[lat, :levels] = jnp.where(masked, 0.0, areas * wrap)
    part[lat, levels:] = areas

    def take_back():
        wait(back, b_sem.at[1], peers)
        total = jnp.zeros((levels, LANES), jnp.float32)
        sub = lax.broadcasted_iota(jnp.int32, (levels, LANES), 0)
        for l in range(levels):
            total = jnp.where(sub == l, back[l, halves * POLAR : halves * POLAR + 1, :], total)
        first_lane = lane_index((levels, LANES)) == 0
        part[lat, :levels, :LANES] = part[lat, :levels, :LANES] + jnp.where(first_lane, total, 0.0)

    def send_part():
        @pl.loop(1, z)
        def _(k):
            send(part.at[lat], part.at[lat], d_sem, k, "lat")

    pl.when(jnp.logical_not(polar))(send_part)

    @pl.loop(0, levels, step=GROUP)
    def _(first):
        @pl.when(polar & (first == GROUP))
        def _():
            take_back()
            send_part()

        for l in range(GROUP):
            flow = bg[first + l] * entry[pl.ds(first + l, 1), :] + bo[first + l]
            for v in range(steps):
                ct[first + l, pl.ds(v, CHUNKS, stride=steps), :] = gs[v, first + l] * flow + os[v, first + l]
            for h in range(halves):
                c = pl.ds(h * LANES, LANES)
                updated[first + l, :, c] = jnp.transpose(ct[first + l, c, :]) * cov[first + l, :, c]

    @pl.when(polar)
    def _():
        for l in range(levels):
            for h in range(halves):
                updated[l, slab, pl.ds(h * LANES, LANES)] = back[l, h * POLAR : (h + 1) * POLAR, :]
        wait(slabs, p_sem.at[0], peers)
        is_worker(me, lambda: wait(pu, b_sem.at[0], n - 1))

    wait(maps, m_sem.at[0], n - 1)
    wait(part, d_sem.at[0], z - 1)
    wait(part, d_sem.at[1], z - 1)
    total = part[0]
    for s in range(1, z):
        total = total + part[s]
    sums = jnp.sum(total, axis=1, keepdims=True)
    mean = jnp.broadcast_to(sums[:levels] / sums[levels:], (levels, LANES))
    diagonal = lax.broadcasted_iota(jnp.int32, (levels, LANES), 0) == lane_index((levels, LANES))
    dateline[...] = jnp.sum(jnp.where(diagonal, mean, 0.0), axis=0, keepdims=True)[:, :levels]


def write_out(updated_in, dateline_in, updated, dateline, sem):
    copies = (
        pltpu.make_async_copy(updated_in, updated, sem.at[0]),
        pltpu.make_async_copy(dateline_in, dateline, sem.at[1]),
    )
    for copy in copies:
        copy.start()
    for copy in copies:
        copy.wait()


def body(n, z, tracer, courant, hop_counts, row_area):
    levels, rows, cells = tracer.shape
    f32 = jnp.float32
    vmem = pl.BlockSpec(memory_space=pltpu.VMEM)
    hbm = pl.BlockSpec(memory_space=pl.ANY)
    dma = pltpu.SemaphoreType.DMA
    inputs = (tracer, courant, hop_counts.reshape(1, rows), row_area.reshape(1, rows))
    updated, dateline = pl.pallas_call(
        functools.partial(kernel, n, z),
        out_shape=(
            pltpu.VMEM(tracer.shape, f32),
            pltpu.VMEM((1, levels), f32),
        ),
        in_specs=[hbm] * 4,
        out_specs=(vmem, vmem),
        scratch_shapes=[
            pltpu.VMEM(tracer.shape, f32),
            pltpu.VMEM(tracer.shape, f32),
            pltpu.VMEM((levels, cells, rows), f32),
            pltpu.VMEM((levels, cells, rows), f32),
            pltpu.VMEM((cells // CHUNKS, levels, CHUNKS, rows), f32),
            pltpu.VMEM((cells // CHUNKS, levels, CHUNKS, rows), f32),
            pltpu.VMEM((levels, CHUNKS, rows), f32),
            pltpu.VMEM((levels, CHUNKS, rows), f32),
            pltpu.VMEM((levels, rows), f32),
            pltpu.VMEM((n, 2 * levels, rows), f32),
            pltpu.VMEM((levels, 2, POLAR, cells), f32),
            pltpu.VMEM((n, 2, POLAR, cells), f32),
            pltpu.VMEM((n, (cells // LANES + 1) * POLAR, LANES), f32),
            pltpu.VMEM((levels, (cells // LANES + 1) * POLAR, LANES), f32),
            pltpu.VMEM((z, 2 * levels, rows), f32),
            pltpu.VMEM((1, rows), jnp.int32),
            pltpu.VMEM((1, rows), f32),
            dma((2,)), dma((2, levels)), dma((2,)),
            dma((2,)), dma((2,)), dma((2,)), dma((2,)),
        ],
        compiler_params=pltpu.CompilerParams(
            collective_id=0, has_side_effects=True, vmem_limit_bytes=24 * 1024 * 1024
        ),
        cost_estimate=pl.CostEstimate(
            flops=60 * tracer.size, bytes_accessed=12 * tracer.size, transcendentals=tracer.size
        ),
    )(*(pltpu.with_memory_space_constraint(a, pltpu.HBM) for a in inputs))
    held = (pltpu.with_memory_space_constraint(a, pltpu.VMEM) for a in (updated, dateline))
    updated, dateline = pl.pallas_call(
        write_out,
        out_shape=(pltpu.HBM(tracer.shape, f32), pltpu.HBM((1, levels), f32)),
        in_specs=[hbm, hbm],
        out_specs=(hbm, hbm),
        scratch_shapes=[dma((2,))],
    )(*held)
    return updated, dateline.reshape(levels)


def solution(mesh):
    return jax.shard_map(
        functools.partial(body, mesh.shape["lon"], mesh.shape["lat"]),
        mesh=mesh,
        in_specs=(P(None, "lat", "lon"), P(None, "lat", "lon"), P("lat"), P("lat")),
        out_specs=(P(None, "lat", "lon"), P()),
        check_vma=False,
    )
```
